512 devices in a mesh: tm: 16 (over z), space: 32 (over y, x, core).
Axes of the slice: x: 4, y: 4, z: 16, core: 2. Of those that a mesh axis runs over, the one named last changes fastest.
Arguments:
- c_points: float32 [16, 5, 2048, 512], P('tm', None, 'space'), may hold values from -6 to 6
- terminal: float32 [5, 2048, 512], P(None, 'space'), may hold values from -6 to 6
- forcing: bfloat16 [16, 4, 5, 2048, 512], P('tm', None, None, 'space'), may hold values from -4 to 4
- conductance: float32 [2048, 512], P('space'), may hold values from 0.05 to 0.25
- coupling: float32 [5, 5], replicated
- flap_cells: int32 [1024, 128], P('space'), may hold values from -1 to 32767, as said below
- flap_actuator: int32 [1024, 128], P('space'), may hold values from -1 to 3, as said below
- flap_area: float32 [1024, 128], P('space'), may hold values from 0.5 to 2
- actuator_rate: float32 [128], P('space'), may hold values from 0.0046875 to 0.046875
Outputs:
- new_points: float32 [16, 5, 2048, 512], P('tm', None, 'space')
- actuator_adjoint: float32 [16, 4, 128], P('tm', None, 'space')
The draws below stay inside these ranges and needn't reach their ends.
Inputs may be any that keep to these rules, and one draw needn't show every extreme that they name: `flap_cells`: empty slots hold -1; every live slot names a cell of the sending device's block. One owner gets 128 live slots from every device; other devices may send nothing. Each device's full tile names its last cell in some slot. `flap_actuator`: -1 exactly where flap_cells is -1, else an actuator of the owner.
All inputs are finite; a program needn't handle non-finite values.
Results may differ from the reference program's by a relative error of at most 0.00105.
Values may be sent and summed in bfloat16 or wider, within the bound.
A program may use at most 64 MiB of HBM per device.

```python
import math
import jax
import jax.numpy as jnp
from jax import lax

FIELDS = 5
STEPS = 4
COLS = 512
ROW_DEV = 64
CAP = 128
ACT_DEV = 4
ROWS = 2048
ACTS = 128
N_TM = 16
N_SPACE = 32


def flap_layout(key):
    first, second, third = jax.random.split(key, 3)
    raw = jax.random.randint(first, (N_SPACE, N_SPACE), 0, 2 * CAP)
    active = jax.random.randint(second, (N_SPACE, 1), 0, 2)
    full_dest = jax.random.randint(third, (), 0, N_SPACE)
    dest = jnp.arange(N_SPACE)[None, :]
    counts = jnp.where(dest == full_dest, CAP, jnp.minimum(raw, CAP) * active)
    slot = jnp.arange(CAP)[None, None, :]
    live = slot < counts[:, :, None]
    return live.reshape(N_SPACE * N_SPACE, CAP)


def full_corner(live):
    slot = jnp.arange(CAP)[None, :]
    return jnp.logical_and(live, slot == CAP - 1)


def draw_flap_cells(key, part):
    live = flap_layout(key)
    key = jax.random.fold_in(key, 11)
    cells = jax.random.randint(key, live.shape, 0, ROW_DEV * COLS)
    cells = jnp.where(full_corner(live), ROW_DEV * COLS - 1, cells)
    return jnp.where(live, cells, -1).astype(jnp.int32)


def draw_flap_actuator(key, part):
    live = flap_layout(key)
    key = jax.random.fold_in(key, 23)
    ids = jax.random.randint(key, live.shape, 0, ACT_DEV)
    ids = jnp.where(full_corner(live), ACT_DEV - 1, ids)
    return jnp.where(live, ids, -1).astype(jnp.int32)


def draw_coupling(key, part):
    key = jax.random.fold_in(key, 5)
    noise = jax.random.normal(key, (FIELDS, FIELDS), jnp.float32) * 0.08
    ident = jnp.eye(FIELDS, dtype=jnp.float32)
    return (0.85 * ident + noise * (1.0 - ident)).astype(jnp.float32)


def block_scale(rng, shape, pieces, smallest, high):
    def one(dim, parts):
        draws = jax.random.uniform(jax.random.fold_in(jax.random.fold_in(rng, 6), dim), (parts,), jnp.float32, smallest / len(pieces), high / len(pieces))
        return jnp.repeat(jnp.exp(draws), shape[dim] // parts).reshape((-1,) + (1,) * (len(shape) - dim - 1))

    gain = one(*pieces[0])
    for cut in pieces[1:]:
        gain = gain * one(*cut)
    return gain


def bell_draw(own_key, dims, spread, limit, cuts=(), kind=jnp.bfloat16):
    loudness = block_scale(own_key, dims, cuts, -0.22, 0.18) if cuts else 1.0
    values = jax.random.normal(own_key, dims, jnp.float32) * spread * loudness
    return jnp.minimum(jnp.maximum(values, -limit), limit).astype(kind)


def setup_inputs(seed: int = 0) -> dict:
    splits = jax.random.split(jax.random.key(seed), 10)
    return {
        "c_points": bell_draw(splits[0], (N_TM, FIELDS, ROWS, COLS), 1.0, 6.0, ((0, 16), (2, 32)), jnp.float32),
        "terminal": bell_draw(splits[1], (FIELDS, ROWS, COLS), 1.0, 6.0, ((1, 32),), jnp.float32),
        "forcing": bell_draw(splits[2], (N_TM, STEPS, FIELDS, ROWS, COLS), 0.5, 4.0, ((0, 16), (3, 32))),
        "conductance": jnp.clip(jnp.exp(math.log(0.25) - 1.609438 * jax.random.uniform(splits[3], (ROWS, COLS), jnp.float32) ** block_scale(splits[3], (ROWS, COLS), ((0, 32),), -0.2, 0.2)), 0.05, 0.25),
        "coupling": draw_coupling(jax.random.fold_in(splits[9], 71), 0),
        "flap_cells": draw_flap_cells(jax.random.fold_in(splits[9], 71), 0),
        "flap_actuator": draw_flap_actuator(jax.random.fold_in(splits[9], 71), 0),
        "flap_area": jnp.clip(jnp.exp(math.log(2.0) - 1.3862944 * jax.random.uniform(splits[7], (N_SPACE * N_SPACE, CAP), jnp.float32) ** block_scale(splits[7], (N_SPACE * N_SPACE, CAP), ((0, 32),), -0.2, 0.2)), 0.5, 2.0),
        "actuator_rate": jnp.clip(jnp.exp(math.log(0.046875) - 2.3025851 * jax.random.uniform(splits[8], (ACTS,), jnp.float32) ** block_scale(splits[8], (ACTS,), ((0, 32),), -0.2, 0.2)), 0.0046875, 0.046875),
    }


def advance(lam, conductance, coupling):
    padded = jnp.pad(lam, ((0, 0), (1, 1), (1, 1)))
    north = padded[:, :-2, 1:-1]
    south = padded[:, 2:, 1:-1]
    west = padded[:, 1:-1, :-2]
    east = padded[:, 1:-1, 2:]
    beside = 0.35 * north + 0.15 * south + 0.3 * west + 0.2 * east
    mixed = lam + conductance * (beside - lam)
    return jnp.einsum("gf,grc->frc", coupling, mixed, precision=lax.Precision.HIGHEST)


def face_loads(lam, flap_cells, flap_actuator, flap_area):
    energy = lam[4].reshape(N_SPACE, ROW_DEV * COLS)
    cells = flap_cells.reshape(N_SPACE, N_SPACE * CAP)
    live = cells >= 0
    picked = jnp.take_along_axis(energy, jnp.maximum(cells, 0), axis=1)
    values = jnp.where(live, picked * flap_area.reshape(N_SPACE, N_SPACE * CAP), 0.0)
    owner = (jnp.arange(N_SPACE * CAP, dtype=jnp.int32) // CAP)[None, :]
    target = jnp.where(live, owner * ACT_DEV + flap_actuator.reshape(N_SPACE, N_SPACE * CAP), ACTS)
    summed = jax.ops.segment_sum(values.reshape(-1), target.reshape(-1).astype(jnp.int32), num_segments=ACTS + 1)
    return summed[:ACTS]


def reference(c_points, terminal, forcing, conductance, coupling, flap_cells, flap_actuator, flap_area, actuator_rate):
    new_list = []
    load_list = []
    for group in range(N_TM):
        lam = terminal if group == N_TM - 1 else c_points[group + 1]
        group_loads = [None] * STEPS
        for step in reversed(range(STEPS)):
            lam = advance(lam, conductance, coupling) + forcing[group, step].astype(jnp.float32)
            group_loads[step] = face_loads(lam, flap_cells, flap_actuator, flap_area)
        new_list.append(lam)
        load_list.append(jnp.stack(group_loads))
    loads = jnp.stack(load_list).reshape(N_TM * STEPS, ACTS)
    decay = jnp.exp(-actuator_rate)

    def backward(carry, load):
        carry = decay * carry + load
        return carry, carry

    _, states = lax.scan(backward, jnp.zeros((ACTS,), jnp.float32), loads, reverse=True)
    return jnp.stack(new_list), states.reshape(N_TM, STEPS, ACTS)
```

```python
import jax
import jax.numpy as jnp
from jax import lax
from jax.experimental import pallas as pl
from jax.experimental.pallas import tpu as pltpu
from jax.sharding import PartitionSpec as P

STEPS = 4
ACT = 4
FIELDS = 5
ROWS = 64
COLS = 512
LANES = 128
BLOCKS = COLS // LANES
CHUNK = 16
CHUNKS = ROWS // CHUNK
EXT = ROWS + 2 * CHUNK
MESH = pl.DeviceIdType.MESH
LEVELS = 32767.0


def quantize(src, rows_at, dst, scales):
    for piece in range(CHUNKS):
        tile = []
        for f in range(FIELDS):
            x = src[f, pl.ds(piece * CHUNK, CHUNK), :]
            top = jnp.max(jnp.abs(x), axis=(0, 1), keepdims=True)
            safe = jnp.maximum(top, 1e-30)
            y = jnp.round(x * (LEVELS / safe))
            dst[f, pl.ds(rows_at + piece * CHUNK, CHUNK), :] = y.astype(jnp.int32).astype(jnp.int16)
            tile.append(jnp.broadcast_to(safe * (1.0 / LEVELS), (1, LANES)))
        tile += [jnp.zeros((1, LANES), jnp.float32)] * (8 - FIELDS)
        scales[piece] = jnp.concatenate(tile, axis=0)


def exchange(
    points, terminal, forcing, conductance,
    start, scale, force_halo, cond_halo,
    raw, coded, coded_scale, end_scale,
    raw_sem, z_send, z_recv, s_send, s_recv,
):
    nt, ns = lax.axis_size("tm"), lax.axis_size("space")
    t, s = lax.axis_index("tm"), lax.axis_index("space")
    barrier = pltpu.get_barrier_semaphore()
    for dev in (
        (lax.rem(t + nt - 1, nt), s), (lax.rem(t + 1, nt), s),
        (t, lax.rem(s + ns - 1, ns)), (t, lax.rem(s + 1, ns)),
    ):
        pl.semaphore_signal(barrier, inc=1, device_id=dev, device_id_type=MESH)
    load = pltpu.make_async_copy(points.at[0], raw, raw_sem)
    load.start()
    load.wait()
    quantize(raw, 0, coded, coded_scale)
    pl.semaphore_wait(barrier, 4)

    def z_copy(src, dst, i):
        return pltpu.make_async_remote_copy(
            src_ref=src, dst_ref=dst, send_sem=z_send.at[i], recv_sem=z_recv.at[i],
            device_id=(t - 1, s), device_id_type=MESH,
        )

    z_copies = [z_copy(coded_scale, scale.at[pl.ds(1, CHUNKS)], CHUNKS)] + [
        z_copy(
            coded.at[:, pl.ds(p * CHUNK, CHUNK), :],
            start.at[:, pl.ds((p + 1) * CHUNK, CHUNK), :], p,
        )
        for p in (CHUNKS - 1, 0, 1, 2)
    ]

    def s_copy(src, dst, i, to):
        return pltpu.make_async_remote_copy(
            src_ref=src, dst_ref=dst, send_sem=s_send.at[i], recv_sem=s_recv.at[i],
            device_id=(t, to), device_id_type=MESH,
        )

    up_first = [
        s_copy(conductance.at[pl.ds(ROWS - 8, 8)], cond_halo.at[0], 0, s + 1),
        s_copy(
            forcing.at[0, pl.ds(1, 3), :, pl.ds(ROWS - CHUNK, CHUNK), :], force_halo.at[0], 1, s + 1
        ),
    ]
    down_first = [
        s_copy(conductance.at[pl.ds(0, 8)], cond_halo.at[1], 4, s - 1),
        s_copy(forcing.at[0, pl.ds(1, 3), :, pl.ds(0, CHUNK), :], force_halo.at[1], 5, s - 1),
    ]
    up_then = [
        s_copy(scale.at[CHUNKS], scale.at[0], 2, s + 1),
        s_copy(
            start.at[:, pl.ds(ROWS, CHUNK), :], start.at[:, pl.ds(0, CHUNK), :], 3, s + 1
        ),
    ]
    down_then = [
        s_copy(scale.at[1], scale.at[CHUNKS + 1], 6, s - 1),
        s_copy(
            start.at[:, pl.ds(CHUNK, CHUNK), :],
            start.at[:, pl.ds(ROWS + CHUNK, CHUNK), :], 7, s - 1,
        ),
    ]
    has_up, has_down = s < ns - 1, s > 0

    @pl.when(t > 0)
    def _():
        for copy in z_copies:
            copy.start()

    @pl.when(has_up)
    def _():
        for copy in up_first:
            copy.start()

    @pl.when(has_down)
    def _():
        for copy in down_first:
            copy.start()

    @pl.when(t == nt - 1)
    def _():
        end = pltpu.make_async_copy(terminal, raw, raw_sem)
        end.start()
        end.wait()
        quantize(raw, CHUNK, start, end_scale)
        for p in range(CHUNKS):
            scale[p + 1] = end_scale[p]

    @pl.when(t < nt - 1)
    def _():
        for copy in z_copies[:2]:
            copy.wait_recv()

    @pl.when(has_up)
    def _():
        for copy in up_then:
            copy.start()

    @pl.when(t < nt - 1)
    def _():
        z_copies[2].wait_recv()

    @pl.when(has_down)
    def _():
        for copy in down_then:
            copy.start()

    @pl.when(jnp.logical_not(has_down))
    def _():
        cond_halo[0] = jnp.zeros((8, COLS), jnp.float32)
        force_halo[0] = jnp.zeros((3, FIELDS, CHUNK, COLS), jnp.bfloat16)
        scale[0] = jnp.zeros((8, LANES), jnp.float32)
        start[:, pl.ds(0, CHUNK), :] = jnp.zeros((FIELDS, CHUNK, COLS), jnp.int16)

    @pl.when(jnp.logical_not(has_up))
    def _():
        cond_halo[1] = jnp.zeros((8, COLS), jnp.float32)
        force_halo[1] = jnp.zeros((3, FIELDS, CHUNK, COLS), jnp.bfloat16)
        scale[CHUNKS + 1] = jnp.zeros((8, LANES), jnp.float32)
        start[:, pl.ds(ROWS + CHUNK, CHUNK), :] = jnp.zeros((FIELDS, CHUNK, COLS), jnp.int16)

    @pl.when(t < nt - 1)
    def _():
        for copy in z_copies[3:]:
            copy.wait_recv()

    @pl.when(has_down)
    def _():
        for copy in up_first + up_then:
            copy.wait_recv()
        for copy in down_first + down_then:
            copy.wait_send()

    @pl.when(has_up)
    def _():
        for copy in down_first + down_then:
            copy.wait_recv()
        for copy in up_first + up_then:
            copy.wait_send()

    @pl.when(t > 0)
    def _():
        for copy in z_copies:
            copy.wait_send()


def one_tile(src, cond, row, coupling, lane):
    first, last = lane == 0, lane == LANES - 1
    weight = [cond[b, pl.ds(row, 8), :] for b in range(BLOCKS)]
    mixed = []
    for f in range(FIELDS):
        mid = [src[f, b, pl.ds(row, 8), :] for b in range(BLOCKS)]
        left = [pltpu.roll(v, 1, 1) for v in mid]
        right = [pltpu.roll(v, LANES - 1, 1) for v in mid]
        out = []
        for b in range(BLOCKS):
            west = jnp.where(first, left[b - 1] if b else 0.0, left[b])
            east = jnp.where(last, right[b + 1] if b < BLOCKS - 1 else 0.0, right[b])
            north = src[f, b, pl.ds(row - 1, 8), :]
            south = src[f, b, pl.ds(row + 1, 8), :]
            beside = 0.35 * north + 0.15 * south + 0.3 * west + 0.2 * east
            out.append(mid[b] + weight[b] * (beside - mid[b]))
        mixed.append(out)
    result = []
    for f in range(FIELDS):
        row_out = []
        for b in range(BLOCKS):
            total = coupling[0][f] * mixed[0][b]
            for g in range(1, FIELDS):
                total = total + coupling[g][f] * mixed[g][b]
            row_out.append(total)
        result.append(row_out)
    return result


def relax(
    start, scale, forcing, force_halo, conductance, cond_halo, coupling_ref, cells, acts, area,
    points, partial,
    lam_a, lam_b, cond, picked,
):
    lane = lax.broadcasted_iota(jnp.int32, (8, LANES), 1)
    coupling = [[coupling_ref[g, f] for f in range(FIELDS)] for g in range(FIELDS)]

    for b in range(BLOCKS):
        cols = pl.ds(b * LANES, LANES)
        cond[b, pl.ds(8, 8), :] = cond_halo[0, :, cols]
        cond[b, pl.ds(CHUNK, ROWS), :] = conductance[:, cols]
        cond[b, pl.ds(CHUNK + ROWS, 8), :] = cond_halo[1, :, cols]
        for piece in range(CHUNKS + 2):
            rows = pl.ds(piece * CHUNK, CHUNK)
            for f in range(FIELDS):
                factor = scale[piece, f : f + 1, :]
                lam_a[f, b, rows, :] = start[f, rows, cols].astype(jnp.int32).astype(jnp.float32) * factor

    key = lax.shift_right_arithmetic(cells[...], 7)
    slot_lane = jnp.bitwise_and(cells[...], LANES - 1)

    def pick(k, src):
        def body(r, acc):
            for b in range(BLOCKS):
                row = jnp.broadcast_to(src[4, b, pl.ds(CHUNK + r, 1), :], key.shape)
                got = jnp.take_along_axis(row, slot_lane, axis=1, mode="promise_in_bounds")
                acc = jnp.where(key == r * BLOCKS + b, got, acc)
            return acc

        acc = lax.fori_loop(0, ROWS, body, jnp.zeros(key.shape, jnp.float32), unroll=4)
        picked[k] = acc * area[...]

    src, dst = lam_a, lam_b
    for k in reversed(range(STEPS)):
        if k:
            for edge, row in ((0, 8), (1, CHUNK + ROWS)):
                got = one_tile(src, cond, row, coupling, lane)
                for f in range(FIELDS):
                    for b in range(BLOCKS):
                        push = force_halo[edge, k - 1, f, :, pl.ds(b * LANES, LANES)].astype(jnp.float32)
                        push = push[8:] if edge == 0 else push[:8]
                        dst[f, b, pl.ds(row, 8), :] = got[f][b] + push

        def body(j, carry, k=k, src=src, dst=dst):
            for half in range(2):
                at = pl.multiple_of(j * CHUNK, CHUNK)
                row = pl.multiple_of(j * CHUNK + CHUNK + 8 * half, 8)
                got = one_tile(src, cond, row, coupling, lane)
                for f in range(FIELDS):
                    for b in range(BLOCKS):
                        cols = pl.ds(b * LANES, LANES)
                        push = forcing[0, k, f, pl.ds(at, CHUNK), cols].astype(jnp.float32)
                        value = got[f][b] + push[8 * half : 8 * half + 8]
                        if k == 0:
                            points[0, f, pl.ds(at + 8 * half, 8), cols] = value
                        if k or f == 4:
                            dst[f, b, pl.ds(row, 8), :] = value
            return carry

        lax.fori_loop(0, CHUNKS, body, 0)
        pick(k, dst)
        src, dst = dst, src

    ids = acts[...]
    wide = lax.broadcasted_iota(jnp.int32, key.shape, 1)
    total = jnp.zeros(key.shape, jnp.float32)
    for k in range(STEPS):
        values = picked[k]
        for a in range(ACT):
            part = jnp.sum(jnp.where(ids == a, values, 0.0), axis=1, keepdims=True)
            total = jnp.where(jnp.bitwise_and(wide, STEPS * ACT - 1) == k * ACT + a, part, total)
    partial[...] = total.reshape(partial.shape)


def collect(partial, rate, states, mine, later, send, s_send, s_recv, t_send, t_recv):
    nt, ns = lax.axis_size("tm"), lax.axis_size("space")
    t, s = lax.axis_index("tm"), lax.axis_index("space")
    later[...] = jnp.zeros(later.shape, jnp.float32)
    barrier = pltpu.get_barrier_semaphore()

    def greet_space(i, carry):
        pl.semaphore_signal(barrier, inc=1, device_id=(t, lax.rem(s + i, ns)), device_id_type=MESH)
        return carry

    def greet_time(i, carry):
        pl.semaphore_signal(barrier, inc=1, device_id=(lax.rem(t + i, nt), s), device_id_type=MESH)
        return carry

    lax.fori_loop(1, ns, greet_space, 0)
    lax.fori_loop(1, nt, greet_time, 0)
    pl.semaphore_wait(barrier, ns - 1 + nt - 1)

    def to_owner(i):
        d = lax.rem(s + i, ns)
        return pltpu.make_async_remote_copy(
            src_ref=partial.at[d], dst_ref=mine.at[s], send_sem=s_send.at[i], recv_sem=s_recv.at[ns - i],
            device_id=(t, d), device_id_type=MESH,
        )

    lax.fori_loop(1, ns, lambda i, c: (to_owner(i).start(), c)[1], 0)
    mine[s] = partial[s]
    r = rate[...]
    lane = lax.broadcasted_iota(jnp.int32, (1, LANES), 1)
    k_of = lax.rem(lane, STEPS * ACT) // ACT
    k_f = k_of.astype(jnp.float32)
    gap = lax.broadcasted_iota(jnp.int32, later.shape, 0) - t - 1
    weight = jnp.where(gap >= 0, jnp.exp(-(STEPS * 1.0) * gap.astype(jnp.float32) * r[None]), 0.0)
    decay = [jnp.exp(-float(m) * r) for m in range(STEPS)]

    def from_slot(i, c):
        d = lax.rem(s + i, ns)
        pltpu.make_async_remote_copy(
            src_ref=partial.at[d], dst_ref=mine.at[d], send_sem=s_send.at[i], recv_sem=s_recv.at[i],
            device_id=(t, d), device_id_type=MESH,
        ).wait_recv()
        return c

    lax.fori_loop(1, ns, from_slot, 0)
    load = jnp.sum(mine[...], axis=0)
    weighted = load * jnp.exp(-k_f * r)
    for shift in (8, 4):
        weighted = weighted + pltpu.roll(weighted, shift, 1)
    send[...] = weighted

    def earlier(i):
        return pltpu.make_async_remote_copy(
            src_ref=send, dst_ref=later.at[t], send_sem=t_send.at[i], recv_sem=t_recv.at[t],
            device_id=(i, s), device_id_type=MESH,
        )

    lax.fori_loop(0, t, lambda i, c: (earlier(i).start(), c)[1], 0)
    base = load
    for m in range(1, STEPS):
        moved = pltpu.roll(load, LANES - ACT * m, 1)
        base = base + jnp.where(k_of + m < STEPS, decay[m] * moved, 0.0)

    def arrived(i, c):
        pltpu.make_async_remote_copy(
            src_ref=send, dst_ref=later.at[i], send_sem=t_send.at[i], recv_sem=t_recv.at[i],
            device_id=(i, s), device_id_type=MESH,
        ).wait_recv()
        return c

    lax.fori_loop(t + 1, nt, arrived, 0)
    incoming = jnp.sum(later[...] * weight, axis=0)
    states[...] = base + jnp.exp(-(STEPS - k_f) * r) * incoming
    lax.fori_loop(0, t, lambda i, c: (earlier(i).wait_send(), c)[1], 0)
    lax.fori_loop(1, ns, lambda i, c: (to_owner(i).wait_send(), c)[1], 0)


def per_device(
    c_points, terminal, forcing, conductance, coupling, flap_cells, flap_actuator, flap_area, actuator_rate
):
    nt, ns = lax.axis_size("tm"), lax.axis_size("space")
    anywhere = pl.BlockSpec(memory_space=pl.ANY)
    vmem = pl.BlockSpec(memory_space=pltpu.VMEM)
    smem = pl.BlockSpec(memory_space=pltpu.SMEM)
    dma = pltpu.SemaphoreType.DMA
    f32 = jnp.float32
    start, scale, force_halo, cond_halo = pl.pallas_call(
        exchange,
        out_shape=(
            jax.ShapeDtypeStruct((FIELDS, EXT, COLS), jnp.int16),
            jax.ShapeDtypeStruct((CHUNKS + 2, 8, LANES), f32),
            jax.ShapeDtypeStruct((2, STEPS - 1, FIELDS, CHUNK, COLS), jnp.bfloat16),
            jax.ShapeDtypeStruct((2, 8, COLS), f32),
        ),
        in_specs=[anywhere] * 4,
        out_specs=(vmem,) * 4,
        scratch_shapes=[
            pltpu.VMEM((FIELDS, ROWS, COLS), f32),
            pltpu.VMEM((FIELDS, ROWS, COLS), jnp.int16),
            pltpu.VMEM((CHUNKS, 8, LANES), f32),
            pltpu.VMEM((CHUNKS, 8, LANES), f32),
            dma,
            dma((CHUNKS + 1,)), dma((CHUNKS + 1,)), dma((8,)), dma((8,)),
        ],
        compiler_params=pltpu.CompilerParams(
            collective_id=0, has_side_effects=True, vmem_limit_bytes=32 * 2**20
        ),
        name="exchange",
    )(c_points, terminal, forcing, conductance)
    points, partial = pl.pallas_call(
        relax,
        out_shape=(
            jax.ShapeDtypeStruct((1, FIELDS, ROWS, COLS), f32),
            jax.ShapeDtypeStruct((ns, 1, LANES), f32),
        ),
        in_specs=[vmem] * 6 + [smem] + [vmem] * 3,
        out_specs=(vmem, vmem),
        scratch_shapes=[
            pltpu.VMEM((FIELDS, BLOCKS, EXT, LANES), f32),
            pltpu.VMEM((FIELDS, BLOCKS, EXT, LANES), f32),
            pltpu.VMEM((BLOCKS, EXT, LANES), f32),
            pltpu.VMEM((STEPS, ns, LANES), f32),
        ],
        compiler_params=pltpu.CompilerParams(vmem_limit_bytes=32 * 2**20),
        name="relax",
    )(start, scale, forcing, force_halo, conductance, cond_halo, coupling, flap_cells, flap_actuator, flap_area)
    rate = jnp.tile(actuator_rate, LANES // ACT)[None]
    states = pl.pallas_call(
        collect,
        out_shape=jax.ShapeDtypeStruct((1, LANES), f32),
        in_specs=[vmem, vmem],
        out_specs=vmem,
        scratch_shapes=[
            pltpu.VMEM((ns, 1, LANES), f32),
            pltpu.VMEM((nt, 1, LANES), f32),
            pltpu.VMEM((1, LANES), f32),
            dma((ns,)), dma((ns,)), dma((nt,)), dma((nt,)),
        ],
        compiler_params=pltpu.CompilerParams(collective_id=1, has_side_effects=True),
        name="collect",
    )(partial, rate)
    return (points, states[0, : STEPS * ACT].reshape(1, STEPS, ACT))


def solution(mesh):
    placed = (
        P("tm", None, "space", None),
        P(None, "space", None),
        P("tm", None, None, "space", None),
        P("space", None),
        P(),
        P("space", None),
        P("space", None),
        P("space", None),
        P("space"),
    )
    return jax.shard_map(
        per_device,
        mesh=mesh,
        in_specs=placed,
        out_specs=(P("tm", None, "space", None), P("tm", None, "space")),
        check_vma=False,
    )
```

```python
import jax
import jax.numpy as jnp
from jax import lax
from jax.experimental import pallas as pl
from jax.experimental.pallas import tpu as pltpu
from jax.sharding import PartitionSpec as P

STEPS = 4
ACT = 4
FIELDS = 5
ROWS = 64
COLS = 512
LANES = 128
BLOCKS = COLS // LANES
CHUNK = 16
CHUNKS = ROWS // CHUNK
EXT = ROWS + 2 * CHUNK
ORDER = (3, 0, 1, 2)
MESH = pl.DeviceIdType.MESH
LEVELS = 32767.0
f32 = jnp.float32
bf16 = jnp.bfloat16

LEFT = ((3, 13, 39, 5), (2, 14, 38, 4), (1, 15, 37, 4), (0, 16, 36, 4))
RIGHT = ((3, 65, 75, 3), (2, 66, 74, 2), (1, 67, 73, 2), (0, 68, 72, 2))
MIDDLE = ((3, 47, 57, 3), (2, 46, 58, 3), (1, 45, 59, 3), (0, 44, 60, 3))


def quantize(src, piece, dst, row, scales):
    tile = []
    for f in range(FIELDS):
        x = src[f, pl.ds(piece * CHUNK, CHUNK), :]
        top = jnp.max(jnp.abs(x), axis=(0, 1), keepdims=True)
        safe = jnp.maximum(top, 1e-30)
        y = jnp.round(x * (LEVELS / safe))
        dst[f, pl.ds(row, CHUNK), :] = y.astype(jnp.int32).astype(jnp.int16)
        tile.append(jnp.broadcast_to(safe * (1.0 / LEVELS), (1, LANES)))
    tile += [jnp.zeros((1, LANES), f32)] * (8 - FIELDS)
    scales[piece] = jnp.concatenate(tile, axis=0)


def one_tile(src, cond, row, coupling, lane):
    first, last = lane == 0, lane == LANES - 1
    weight = [cond[b, pl.ds(row, 8), :] for b in range(BLOCKS)]
    mixed = []
    for f in range(FIELDS):
        mid = [src[f, b, pl.ds(row, 8), :] for b in range(BLOCKS)]
        left = [pltpu.roll(v, 1, 1) for v in mid]
        right = [pltpu.roll(v, LANES - 1, 1) for v in mid]
        out = []
        for b in range(BLOCKS):
            west = jnp.where(first, left[b - 1] if b else 0.0, left[b])
            east = jnp.where(last, right[b + 1] if b < BLOCKS - 1 else 0.0, right[b])
            north = src[f, b, pl.ds(row - 1, 8), :]
            south = src[f, b, pl.ds(row + 1, 8), :]
            beside = 0.35 * north + 0.15 * south + 0.3 * west + 0.2 * east
            out.append(mid[b] + weight[b] * (beside - mid[b]))
        mixed.append(out)
    result = []
    for f in range(FIELDS):
        row_out = []
        for b in range(BLOCKS):
            total = coupling[0][f] * mixed[0][b]
            for g in range(1, FIELDS):
                total = total + coupling[g][f] * mixed[g][b]
            row_out.append(total)
        result.append(row_out)
    return result


def space_offsets(ns):
    nc = 2
    nx = min(4, ns // nc)
    ny = ns // (nc * nx)
    far = lambda d, n: min(d, n - d)
    steps = [(y, x, c) for y in range(ny) for x in range(nx) for c in range(nc)][1:]
    steps.sort(key=lambda o: -(2 * far(o[0], ny) + 2 * far(o[1], nx) + o[2]))
    return steps, (ny, nx, nc)


def time_offsets(nt):
    return sorted(range(1, nt), key=lambda j: -min(j, nt - j))


def offsets(distances, n):
    return sorted({d % n for d in distances} - {0})


def whole(
    points_in, terminal, forcing, conductance, coupling_ref, cells_in, acts_in, area_in, rate_ref,
    points, states,
    raw, coded, coded_scale, end_scale, start, scale, force_halo, cond_halo,
    force_own, cond_own, cells, acts, area,
    lam, push, cond, column, row_area, energy, picked, partial, mine, later, later_weight, send,
    raw_sem, in_sem, z_send, z_recv, s_send, s_recv, a_send, a_recv, t_send, t_recv,
    greet_y, greet_far, greet_farther,
):
    nt, ns = lax.axis_size("tm"), lax.axis_size("space")
    t, s = lax.axis_index("tm"), lax.axis_index("space")
    around, (ny, nx, nc) = space_offsets(ns)
    place = (s // (nx * nc), lax.rem(s // nc, nx), lax.rem(s, nc))

    def beside(o):
        y, x = lax.rem(place[0] + o[0], ny), lax.rem(place[1] + o[1], nx)
        c = 1 - place[2] if o[2] else place[2]
        return (t, (y * nx + x) * nc + c)

    def inverse(o):
        return around.index(((-o[0]) % ny, (-o[1]) % nx, o[2]))

    def in_time(j):
        return (lax.rem(t + j, nt), s)

    def signal(sem, dev):
        pl.semaphore_signal(sem, inc=1, device_id=dev, device_id_type=MESH)

    raw_loads = [
        pltpu.make_async_copy(
            points_in.at[0, :, pl.ds(p * CHUNK, CHUNK), :], raw.at[:, pl.ds(p * CHUNK, CHUNK), :],
            raw_sem.at[p],
        )
        for p in range(CHUNKS)
    ]
    for p in ORDER:
        raw_loads[p].start()
    later[...] = jnp.zeros(later.shape, f32)
    barrier = pltpu.get_barrier_semaphore()
    near_time = offsets((1, -1, 2, -2), nt)
    near_space = [o for o in around if o[0] == 0 or o[1:] == (0, 0)]
    for j in near_time:
        signal(barrier, in_time(j))
    signal(barrier, (t, lax.rem(s + 1, ns)))
    signal(barrier, (t, lax.rem(s + ns - 1, ns)))
    for o in near_space:
        signal(barrier, beside(o))
    loads = [
        pltpu.make_async_copy(src, dst, in_sem.at[i])
        for i, (src, dst) in enumerate((
            (cells_in, cells), (acts_in, acts), (area_in, area), (conductance, cond_own),
            (forcing.at[0], force_own),
        ))
    ]
    for load in loads:
        load.start()
    for p in ORDER:
        raw_loads[p].wait()
        quantize(raw, p, coded, p * CHUNK, coded_scale)
    pl.semaphore_wait(barrier, len(near_time) + 2 + len(near_space))

    def z_copy(src, dst, i):
        return pltpu.make_async_remote_copy(
            src_ref=src, dst_ref=dst, send_sem=z_send.at[i], recv_sem=z_recv.at[i],
            device_id=(t - 1, s), device_id_type=MESH,
        )

    z_scale = z_copy(coded_scale, scale.at[pl.ds(1, CHUNKS)], CHUNKS)
    z_piece = [
        z_copy(
            coded.at[:, pl.ds(p * CHUNK, CHUNK), :], start.at[:, pl.ds((p + 1) * CHUNK, CHUNK), :], p
        )
        for p in range(CHUNKS)
    ]

    def s_copy(src, dst, i, to):
        return pltpu.make_async_remote_copy(
            src_ref=src, dst_ref=dst, send_sem=s_send.at[i], recv_sem=s_recv.at[i],
            device_id=(t, to), device_id_type=MESH,
        )

    up_first = [
        s_copy(conductance.at[pl.ds(ROWS - 8, 8)], cond_halo.at[0], 0, s + 1),
        s_copy(
            forcing.at[0, pl.ds(1, 3), :, pl.ds(ROWS - CHUNK, CHUNK), :], force_halo.at[0], 1, s + 1
        ),
    ]
    down_first = [
        s_copy(conductance.at[pl.ds(0, 8)], cond_halo.at[1], 4, s - 1),
        s_copy(forcing.at[0, pl.ds(1, 3), :, pl.ds(0, CHUNK), :], force_halo.at[1], 5, s - 1),
    ]
    up_then = [
        s_copy(scale.at[CHUNKS], scale.at[0], 2, s + 1),
        s_copy(start.at[:, pl.ds(ROWS, CHUNK), :], start.at[:, pl.ds(0, CHUNK), :], 3, s + 1),
    ]
    down_then = [
        s_copy(scale.at[1], scale.at[CHUNKS + 1], 6, s - 1),
        s_copy(
            start.at[:, pl.ds(CHUNK, CHUNK), :], start.at[:, pl.ds(ROWS + CHUNK, CHUNK), :], 7, s - 1
        ),
    ]
    has_up, has_down = s < ns - 1, s > 0
    has_later, has_earlier = t < nt - 1, t > 0

    @pl.when(has_earlier)
    def _():
        z_scale.start()
        for p in ORDER:
            z_piece[p].start()

    @pl.when(has_up)
    def _():
        for copy in up_first:
            copy.start()

    @pl.when(has_down)
    def _():
        for copy in down_first:
            copy.start()

    same_x = [o for o in near_space if o[1:] == (0, 0)]
    for o in same_x:
        signal(greet_y, beside(o))
    far = offsets((2, -2), nt)
    for j in far:
        signal(greet_far, in_time(j))

    @pl.when(jnp.logical_not(has_later))
    def _():
        end = pltpu.make_async_copy(terminal, raw, raw_sem.at[0])
        end.start()
        end.wait()
        for p in range(CHUNKS):
            quantize(raw, p, start, (p + 1) * CHUNK, end_scale)
            scale[p + 1] = end_scale[p]

    for load in loads:
        load.wait()

    def slots(p, carry):
        for half in range(2):
            cell = cells[pl.ds(2 * p + half, 1), :]
            lanes = pl.ds(half * LANES, LANES)
            col = jnp.broadcast_to(jnp.bitwise_and(cell, COLS - 1), (COLS, LANES))
            at = lax.broadcasted_iota(jnp.int32, (COLS, LANES), 0)
            column[p, :, lanes] = jnp.where(col == at, 1.0, 0.0).astype(bf16)
            row = jnp.broadcast_to(lax.shift_right_arithmetic(cell, 9), (ROWS, LANES))
            weight = jnp.broadcast_to(area[pl.ds(2 * p + half, 1), :], (ROWS, LANES))
            at = lax.broadcasted_iota(jnp.int32, (ROWS, LANES), 0)
            row_area[p, :, lanes] = jnp.where(row == at, weight, 0.0)
        return carry

    lax.fori_loop(0, ns // 2, slots, 0)

    def widen(i, carry):
        k, f = i // FIELDS, lax.rem(i, FIELDS)
        value = force_own[k, f].astype(f32)
        for b in range(BLOCKS):
            push[k, f, b, pl.ds(CHUNK, ROWS), :] = value[:, b * LANES : (b + 1) * LANES]
        return carry

    lax.fori_loop(0, STEPS * FIELDS, widen, 0)
    for b in range(BLOCKS):
        cond[b, pl.ds(CHUNK, ROWS), :] = cond_own[:, pl.ds(b * LANES, LANES)]

    lane1 = lax.broadcasted_iota(jnp.int32, (1, LANES), 1)
    rate = jnp.zeros((1, LANES), f32)
    for a in range(ACT):
        rate = jnp.where(lax.rem(lane1, ACT) == a, rate_ref[a], rate)
    for j in range(1, nt):
        later_weight[j] = jnp.exp(-float(STEPS * (j - 1)) * rate)
    later_weight[0] = jnp.zeros((1, LANES), f32)

    lane = lax.broadcasted_iota(jnp.int32, (8, LANES), 1)
    coupling = [[coupling_ref[g, f] for f in range(FIELDS)] for g in range(FIELDS)]

    def decode(piece):
        rows = pl.ds(piece * CHUNK, CHUNK)
        for f in range(FIELDS):
            value = start[f, rows, :].astype(jnp.int32).astype(f32)
            factor = scale[piece, f : f + 1, :]
            for b in range(BLOCKS):
                lam[0, f, b, rows, :] = value[:, b * LANES : (b + 1) * LANES] * factor

    def windows(parts):
        for k, first, last, count in parts:
            def body(i, carry, k=k, first=first, last=last):
                row = jnp.minimum(first + 8 * i, last)
                got = one_tile(lam.at[STEPS - 1 - k], cond, row, coupling, lane)
                for f in range(FIELDS):
                    for b in range(BLOCKS):
                        lam[STEPS - k, f, b, pl.ds(row, 8), :] = (
                            got[f][b] + push[k, f, b, pl.ds(row, 8), :]
                        )
                return carry

            lax.fori_loop(0, count, body, 0)

    @pl.when(has_later)
    def _():
        z_scale.wait_recv()
        z_piece[3].wait_recv()

    @pl.when(has_up)
    def _():
        for copy in up_then:
            copy.start()

    decode(4)

    @pl.when(has_later)
    def _():
        z_piece[0].wait_recv()

    @pl.when(has_down)
    def _():
        for copy in down_then:
            copy.start()

    decode(1)
    pl.semaphore_wait(greet_far, len(far))
    farther = offsets((4, -4), nt)
    for j in farther:
        signal(greet_farther, in_time(j))

    @pl.when(jnp.logical_not(has_down))
    def _():
        cond_halo[0] = jnp.zeros((8, COLS), f32)
        force_halo[0] = jnp.zeros((3, FIELDS, CHUNK, COLS), bf16)
        scale[0] = jnp.zeros((8, LANES), f32)
        start[:, pl.ds(0, CHUNK), :] = jnp.zeros((FIELDS, CHUNK, COLS), jnp.int16)

    @pl.when(jnp.logical_not(has_up))
    def _():
        cond_halo[1] = jnp.zeros((8, COLS), f32)
        force_halo[1] = jnp.zeros((3, FIELDS, CHUNK, COLS), bf16)
        scale[CHUNKS + 1] = jnp.zeros((8, LANES), f32)
        start[:, pl.ds(ROWS + CHUNK, CHUNK), :] = jnp.zeros((FIELDS, CHUNK, COLS), jnp.int16)

    @pl.when(has_down)
    def _():
        for copy in up_first:
            copy.wait_recv()

    @pl.when(has_up)
    def _():
        for copy in down_first:
            copy.wait_recv()

    for edge, row in ((0, 8), (1, CHUNK + ROWS)):
        for b in range(BLOCKS):
            cond[b, pl.ds(row, 8), :] = cond_halo[edge, :, pl.ds(b * LANES, LANES)]
        for k in range(1, STEPS):
            for f in range(FIELDS):
                value = force_halo[edge, k - 1, f].astype(f32)
                value = value[8:] if edge == 0 else value[:8]
                for b in range(BLOCKS):
                    push[k, f, b, pl.ds(row, 8), :] = value[:, b * LANES : (b + 1) * LANES]

    @pl.when(has_later)
    def _():
        z_piece[1].wait_recv()

    decode(2)

    @pl.when(has_down)
    def _():
        for copy in up_then:
            copy.wait_recv()

    decode(0)
    windows(LEFT)

    @pl.when(has_up)
    def _():
        for copy in down_then:
            copy.wait_recv()

    decode(5)
    windows(RIGHT)

    @pl.when(has_later)
    def _():
        z_piece[2].wait_recv()

    decode(3)
    windows(MIDDLE)

    out = []
    for b in range(BLOCKS):
        copy = pltpu.make_async_copy(
            lam.at[STEPS, :, b, pl.ds(CHUNK, ROWS), :], points.at[0, :, :, pl.ds(b * LANES, LANES)],
            raw_sem.at[b],
        )
        copy.start()
        out.append(copy)
    for k in range(STEPS):
        value = jnp.concatenate(
            [lam[STEPS - k, 4, b, pl.ds(CHUNK, ROWS), :] for b in range(BLOCKS)], axis=1
        )
        high = value.astype(bf16)
        energy[pl.ds(2 * k * ROWS, ROWS), :] = high
        energy[pl.ds((2 * k + 1) * ROWS, ROWS), :] = (value - high.astype(f32)).astype(bf16)

    def pick(p, carry):
        got = jnp.dot(energy[...], column[p], preferred_element_type=f32)
        weight = row_area[p]
        for k in range(STEPS):
            at = 2 * k * ROWS
            both = (got[at : at + ROWS] + got[at + ROWS : at + 2 * ROWS]) * weight
            line = jnp.sum(both, axis=0, keepdims=True)
            for half in range(2):
                picked[k, pl.ds(2 * p + half, 1), :] = line[:, half * LANES : (half + 1) * LANES]
        return carry

    lax.fori_loop(0, ns // 2, pick, 0)
    ids = acts[...]
    wide = lax.broadcasted_iota(jnp.int32, ids.shape, 1)
    total = jnp.zeros(ids.shape, f32)
    for k in range(STEPS):
        values = picked[k]
        for a in range(ACT):
            part = jnp.sum(jnp.where(ids == a, values, 0.0), axis=1, keepdims=True)
            total = jnp.where(jnp.bitwise_and(wide, STEPS * ACT - 1) == k * ACT + a, part, total)
    partial[...] = total.reshape(partial.shape)

    pl.semaphore_wait(greet_y, len(same_x))
    to_owner = []
    for i, o in enumerate(around):
        dev = beside(o)
        to_owner.append(pltpu.make_async_remote_copy(
            src_ref=partial.at[dev[1]], dst_ref=mine.at[inverse(o)],
            send_sem=a_send.at[i], recv_sem=a_recv.at[inverse(o)],
            device_id=dev, device_id_type=MESH,
        ))
    for copy in to_owner:
        copy.start()
    mine[ns - 1] = partial[s]
    k_of = lax.rem(lane1, STEPS * ACT) // ACT
    k_f = k_of.astype(f32)
    decay = [jnp.exp(-float(m) * rate) for m in range(STEPS)]
    pl.semaphore_wait(greet_farther, len(farther))
    for i, o in enumerate(around):
        pltpu.make_async_remote_copy(
            src_ref=partial.at[s], dst_ref=mine.at[i], send_sem=a_send.at[i], recv_sem=a_recv.at[i],
            device_id=beside(o), device_id_type=MESH,
        ).wait_recv()
    load = jnp.sum(mine[...], axis=0)
    weighted = load * jnp.exp(-k_f * rate)
    for shift in (8, 4):
        weighted = weighted + pltpu.roll(weighted, shift, 1)
    send[...] = weighted

    to_earlier = {
        j: pltpu.make_async_remote_copy(
            src_ref=send, dst_ref=later.at[j], send_sem=t_send.at[j], recv_sem=t_recv.at[j],
            device_id=(t - j, s), device_id_type=MESH,
        )
        for j in time_offsets(nt)
    }
    for j, copy in to_earlier.items():
        pl.when(t >= j)(copy.start)
    base = load
    for m in range(1, STEPS):
        moved = pltpu.roll(load, LANES - ACT * m, 1)
        base = base + jnp.where(k_of + m < STEPS, decay[m] * moved, 0.0)
    for j, copy in to_earlier.items():
        pl.when(t + j < nt)(copy.wait_recv)
    incoming = jnp.sum(later[...] * later_weight[...], axis=0)
    result = base + jnp.exp(-(STEPS - k_f) * rate) * incoming
    for k in range(STEPS):
        moved = pltpu.roll(result, LANES - ACT * k, 1) if k else result
        states[0, pl.ds(k, 1), :] = moved[:, :ACT]

    for j, copy in to_earlier.items():
        pl.when(t >= j)(copy.wait_send)
    for copy in to_owner:
        copy.wait_send()

    @pl.when(has_up)
    def _():
        for copy in up_first + up_then:
            copy.wait_send()

    @pl.when(has_down)
    def _():
        for copy in down_first + down_then:
            copy.wait_send()

    @pl.when(has_earlier)
    def _():
        z_scale.wait_send()
        for copy in z_piece:
            copy.wait_send()

    for copy in out:
        copy.wait()


def per_device(
    c_points, terminal, forcing, conductance, coupling, flap_cells, flap_actuator, flap_area, actuator_rate
):
    nt, ns = lax.axis_size("tm"), lax.axis_size("space")
    anywhere = pl.BlockSpec(memory_space=pl.ANY)
    vmem = pl.BlockSpec(memory_space=pltpu.VMEM)
    smem = pl.BlockSpec(memory_space=pltpu.SMEM)
    dma = pltpu.SemaphoreType.DMA
    regular = pltpu.SemaphoreType.REGULAR
    i32 = jnp.int32
    points, states = pl.pallas_call(
        whole,
        out_shape=(
            jax.ShapeDtypeStruct((1, FIELDS, ROWS, COLS), f32),
            jax.ShapeDtypeStruct((1, STEPS, ACT), f32),
        ),
        in_specs=[anywhere] * 4 + [smem] + [anywhere] * 3 + [smem],
        out_specs=(anywhere, vmem),
        scratch_shapes=[
            pltpu.VMEM((FIELDS, ROWS, COLS), f32),
            pltpu.VMEM((FIELDS, ROWS, COLS), jnp.int16),
            pltpu.VMEM((CHUNKS, 8, LANES), f32),
            pltpu.VMEM((CHUNKS, 8, LANES), f32),
            pltpu.VMEM((FIELDS, EXT, COLS), jnp.int16),
            pltpu.VMEM((CHUNKS + 2, 8, LANES), f32),
            pltpu.VMEM((2, STEPS - 1, FIELDS, CHUNK, COLS), bf16),
            pltpu.VMEM((2, 8, COLS), f32),
            pltpu.VMEM((STEPS, FIELDS, ROWS, COLS), bf16),
            pltpu.VMEM((ROWS, COLS), f32),
            pltpu.VMEM((ns, LANES), i32),
            pltpu.VMEM((ns, LANES), i32),
            pltpu.VMEM((ns, LANES), f32),
            pltpu.VMEM((STEPS + 1, FIELDS, BLOCKS, EXT, LANES), f32),
            pltpu.VMEM((STEPS, FIELDS, BLOCKS, EXT, LANES), f32),
            pltpu.VMEM((BLOCKS, EXT, LANES), f32),
            pltpu.VMEM((ns // 2, COLS, 2 * LANES), bf16),
            pltpu.VMEM((ns // 2, ROWS, 2 * LANES), f32),
            pltpu.VMEM((2 * STEPS * ROWS, COLS), bf16),
            pltpu.VMEM((STEPS, ns, LANES), f32),
            pltpu.VMEM((ns, 1, LANES), f32),
            pltpu.VMEM((ns, 1, LANES), f32),
            pltpu.VMEM((nt, 1, LANES), f32),
            pltpu.VMEM((nt, 1, LANES), f32),
            pltpu.VMEM((1, LANES), f32),
            dma((CHUNKS,)), dma((5,)), dma((CHUNKS + 1,)), dma((CHUNKS + 1,)), dma((8,)), dma((8,)),
            dma((ns,)), dma((ns,)), dma((nt,)), dma((nt,)),
            regular, regular, regular,
        ],
        compiler_params=pltpu.CompilerParams(
            collective_id=0, has_side_effects=True, vmem_limit_bytes=60 * 2**20
        ),
        name="whole",
    )(c_points, terminal, forcing, conductance, coupling, flap_cells, flap_actuator, flap_area, actuator_rate)
    return (points, states)


def solution(mesh):
    placed = (
        P("tm", None, "space", None),
        P(None, "space", None),
        P("tm", None, None, "space", None),
        P("space", None),
        P(),
        P("space", None),
        P("space", None),
        P("space", None),
        P("space"),
    )
    return jax.shard_map(
        per_device,
        mesh=mesh,
        in_specs=placed,
        out_specs=(P("tm", None, "space", None), P("tm", None, "space")),
        check_vma=False,
    )
```

```python
import jax
import jax.numpy as jnp
from jax import lax
from jax.experimental import pallas as pl
from jax.experimental.pallas import tpu as pltpu
from jax.sharding import PartitionSpec as P

STEPS = 4
ACT = 4
FIELDS = 5
ROWS = 64
COLS = 512
LANES = 128
BLOCKS = COLS // LANES
EDGE = 16
EXT = ROWS + 2 * EDGE
PIECE = 16
PIECES = ROWS // PIECE
GROUP = STEPS * ACT
SETS = 2 * STEPS
MESH = pl.DeviceIdType.MESH
LEVELS = 32767.0
f32 = jnp.float32
bf16 = jnp.bfloat16


def pair(ref, f, b, rows, shift):
    return jnp.concatenate([ref[f, b, pl.ds(row + shift, 8), :] for row in rows], axis=0)


def step_map(src, cond, rows, coupling, lane):
    first, last = lane == 0, lane == LANES - 1
    weight = [
        jnp.concatenate([cond[b, pl.ds(row, 8), :] for row in rows], axis=0) for b in range(BLOCKS)
    ]
    none = jnp.zeros(lane.shape, bf16)
    mixed = []
    for f in range(FIELDS):
        mid = [pair(src, f, b, rows, 0) for b in range(BLOCKS)]
        short = [v.astype(bf16) for v in mid]
        left = [pltpu.roll(v, 1, 1) for v in short]
        right = [pltpu.roll(v, LANES - 1, 1) for v in short]
        out = []
        for b in range(BLOCKS):
            west = jnp.where(first, left[b - 1] if b else none, left[b])
            east = jnp.where(last, right[b + 1] if b < BLOCKS - 1 else none, right[b])
            flat = (jnp.bfloat16(3.0) * west + jnp.bfloat16(2.0) * east).astype(f32)
            north, south = pair(src, f, b, rows, -1), pair(src, f, b, rows, 1)
            beside = 0.35 * north + 0.15 * south + 0.1 * flat
            out.append(mid[b] + weight[b] * (beside - mid[b]))
        mixed.append(out)
    result = []
    for f in range(FIELDS):
        row_out = []
        for b in range(BLOCKS):
            total = coupling[0][f] * mixed[0][b]
            for g in range(1, FIELDS):
                total = total + coupling[g][f] * mixed[g][b]
            row_out.append(total)
        result.append(row_out)
    return result


def space_offsets(ns):
    nc = 2
    nx = min(4, ns // nc)
    ny = ns // (nc * nx)
    far = lambda d, n: min(d, n - d)
    steps = [(y, x, c) for y in range(ny) for x in range(nx) for c in range(nc)][1:]
    steps.sort(key=lambda o: -(2 * far(o[0], ny) + 2 * far(o[1], nx) + o[2]))
    return steps, (ny, nx, nc)


def time_offsets(nt):
    return sorted(range(1, nt), key=lambda j: -min(j, nt - j))


def offsets(distances, n):
    return sorted({d % n for d in distances} - {0})


def whole(
    points_in, terminal, forcing, conductance, coupling_ref, cells_in, acts_in, area_in, rate_ref,
    points, states,
    free, forced, push, cond, force_own, force_out, force_in, cells, acts, area,
    coded, coded_scale, got, got_scale,
    column, row_area, energy, picked, partial, mine, later, later_weight, send,
    in_sem, z_send, z_recv, s_send, s_recv, a_send, a_recv, t_send, t_recv,
    greet_y, greet_far, greet_farther,
):
    nt, ns = lax.axis_size("tm"), lax.axis_size("space")
    t, s = lax.axis_index("tm"), lax.axis_index("space")
    around, (ny, nx, nc) = space_offsets(ns)
    place = (s // (nx * nc), lax.rem(s // nc, nx), lax.rem(s, nc))
    has_up, has_down = s < ns - 1, s > 0
    has_later, has_earlier = t < nt - 1, t > 0
    is_last = jnp.logical_not(has_later)

    def beside(o):
        y, x = lax.rem(place[0] + o[0], ny), lax.rem(place[1] + o[1], nx)
        c = 1 - place[2] if o[2] else place[2]
        return (t, (y * nx + x) * nc + c)

    def inverse(o):
        return around.index(((-o[0]) % ny, (-o[1]) % nx, o[2]))

    def in_time(j):
        return (lax.rem(t + j, nt), s)

    def signal(sem, dev):
        pl.semaphore_signal(sem, inc=1, device_id=dev, device_id_type=MESH)

    own = pl.ds(EDGE, ROWS)

    def load(src, dst, i):
        return pltpu.make_async_copy(src, dst, in_sem.at[i])

    def columns(src, dst, i):
        return [
            load(
                src.at[..., pl.ds(b * LANES, LANES)],
                dst.at[:, b, own, :] if len(dst.shape) == 4 else dst.at[b, own, :], i + b,
            )
            for b in range(BLOCKS)
        ]

    first_loads = columns(points_in.at[0], free.at[0], 0) + columns(conductance, cond, 4)
    force_load = load(forcing.at[0], force_own, 8)
    slot_loads = [load(cells_in, cells, 9), load(acts_in, acts, 10), load(area_in, area, 11)]
    end_loads = columns(terminal, forced.at[0], 12)
    for copy in first_loads + [force_load] + slot_loads:
        copy.start()

    @pl.when(is_last)
    def _():
        for copy in end_loads:
            copy.start()

    later[...] = jnp.zeros(later.shape, f32)
    barrier = pltpu.get_barrier_semaphore()
    near_time = offsets((1, -1, 2, -2), nt)
    near_space = [o for o in around if o[0] == 0 or o[1:] == (0, 0)]
    for j in near_time:
        signal(barrier, in_time(j))
    signal(barrier, (t, lax.rem(s + 1, ns)))
    signal(barrier, (t, lax.rem(s + ns - 1, ns)))
    for o in near_space:
        signal(barrier, beside(o))

    lane16 = lax.broadcasted_iota(jnp.int32, (16, LANES), 1)
    lane1 = lax.broadcasted_iota(jnp.int32, (1, LANES), 1)
    coupling = [[coupling_ref[g, f] for f in range(FIELDS)] for g in range(FIELDS)]

    def advance(src, add, dst, rows):
        value = step_map(src, cond, rows, coupling, lane16)
        for f in range(FIELDS):
            for b in range(BLOCKS):
                for half, row in enumerate(rows):
                    part = value[f][b][8 * half : 8 * half + 8]
                    if add is not None:
                        part = part + add[f, b, pl.ds(row, 8), :]
                    dst[f, b, pl.ds(row, 8), :] = part

    def interior(src, add, dst, j):
        def body(i, carry):
            row = jnp.minimum(EDGE + j + 16 * i, EDGE + ROWS - j - 16)
            advance(src, add, dst, (row, row + 8))
            return carry

        lax.fori_loop(0, ROWS // 16, body, 0)

    def edges(src, add, dst, j):
        advance(src, add, dst, (EDGE - 4 + j, EDGE + ROWS - 4 - j))

    for copy in first_loads:
        copy.wait()
    interior(free.at[0], None, free.at[1], 1)
    interior(free.at[1], None, free.at[2], 2)

    force_load.wait()
    for side, at in ((0, 13), (1, 0)):
        for f in range(FIELDS):
            for k, count, to in ((3, 3, 0), (2, 2, 3), (1, 1, 5)):
                near = force_own[k, f, pl.ds(ROWS - 16 if side == 0 else 0, 16), :].astype(f32)
                near = near[16 - count :] if side == 0 else near[:count]
                for b in range(BLOCKS):
                    force_out[side, f, b, pl.ds(to, count), :] = near[:, b * LANES : (b + 1) * LANES]
            for b in range(BLOCKS):
                force_out[side, f, b, pl.ds(6, 2), :] = jnp.zeros((2, LANES), f32)

    @pl.when(jnp.logical_not(has_down))
    def _():
        free[0, :, :, pl.ds(8, 8), :] = jnp.zeros((FIELDS, BLOCKS, 8, LANES), f32)
        forced[0, :, :, pl.ds(8, 8), :] = jnp.zeros((FIELDS, BLOCKS, 8, LANES), f32)
        cond[:, pl.ds(8, 8), :] = jnp.zeros((BLOCKS, 8, LANES), f32)
        force_in[0] = jnp.zeros((FIELDS, BLOCKS, 8, LANES), f32)

    @pl.when(jnp.logical_not(has_up))
    def _():
        high = pl.ds(EDGE + ROWS, 8)
        free[0, :, :, high, :] = jnp.zeros((FIELDS, BLOCKS, 8, LANES), f32)
        forced[0, :, :, high, :] = jnp.zeros((FIELDS, BLOCKS, 8, LANES), f32)
        cond[:, high, :] = jnp.zeros((BLOCKS, 8, LANES), f32)
        force_in[1] = jnp.zeros((FIELDS, BLOCKS, 8, LANES), f32)

    @pl.when(is_last)
    def _():
        for copy in end_loads:
            copy.wait()

    pl.semaphore_wait(barrier, len(near_time) + 2 + len(near_space))

    def s_copy(src, dst, i, to):
        return pltpu.make_async_remote_copy(
            src_ref=src, dst_ref=dst, send_sem=s_send.at[i], recv_sem=s_recv.at[i],
            device_id=(t, to), device_id_type=MESH,
        )

    def halo(side):
        to = s + 1 if side == 0 else s - 1
        mine_rows = pl.ds(EDGE + ROWS - 8 if side == 0 else EDGE, 8)
        their_rows = pl.ds(8 if side == 0 else EDGE + ROWS, 8)
        i = 4 * side
        return [
            s_copy(free.at[0, :, :, mine_rows, :], free.at[0, :, :, their_rows, :], i, to),
            s_copy(cond.at[:, mine_rows, :], cond.at[:, their_rows, :], i + 1, to),
            s_copy(force_out.at[side], force_in.at[side], i + 2, to),
            s_copy(forced.at[0, :, :, mine_rows, :], forced.at[0, :, :, their_rows, :], i + 3, to),
        ]

    up, down = halo(0), halo(1)
    for has, copies in ((has_up, up), (has_down, down)):
        @pl.when(has)
        def _(copies=copies):
            for copy in copies[:3]:
                copy.start()

        @pl.when(jnp.logical_and(has, is_last))
        def _(copies=copies):
            copies[3].start()

    same_x = [o for o in near_space if o[1:] == (0, 0)]
    for o in same_x:
        signal(greet_y, beside(o))
    far = offsets((2, -2), nt)
    for j in far:
        signal(greet_far, in_time(j))

    interior(free.at[2], None, free.at[3], 3)
    interior(free.at[3], None, free.at[4], 4)

    def widen(i, carry):
        k, f = i // FIELDS, lax.rem(i, FIELDS)
        value = force_own[k, f].astype(f32)
        for b in range(BLOCKS):
            push[k, f, b, own, :] = value[:, b * LANES : (b + 1) * LANES]
        return carry

    lax.fori_loop(0, STEPS * FIELDS, widen, 0)

    @pl.when(has_later)
    def _():
        forced[1, :, :, own, :] = push[3, :, :, own, :]

    @pl.when(is_last)
    def _():
        interior(forced.at[0], push.at[3], forced.at[1], 1)

    pl.semaphore_wait(greet_far, len(far))
    farther = offsets((4, -4), nt)
    for j in farther:
        signal(greet_farther, in_time(j))

    for j in range(2, STEPS + 1):
        interior(forced.at[j - 1], push.at[STEPS - j], forced.at[j], j)

    for copy in slot_loads:
        copy.wait()

    def slots(p, carry):
        for half in range(2):
            cell = cells[pl.ds(2 * p + half, 1), :]
            lanes = pl.ds(half * LANES, LANES)
            col = jnp.broadcast_to(jnp.bitwise_and(cell, COLS - 1), (COLS, LANES))
            at = lax.broadcasted_iota(jnp.int32, (COLS, LANES), 0)
            column[p, :, lanes] = jnp.where(col == at, 1.0, 0.0).astype(bf16)
            row = jnp.broadcast_to(lax.shift_right_arithmetic(cell, 9), (ROWS, LANES))
            weight = jnp.broadcast_to(area[pl.ds(2 * p + half, 1), :], (ROWS, LANES))
            at = lax.broadcasted_iota(jnp.int32, (ROWS, LANES), 0)
            row_area[p, :, lanes] = jnp.where(row == at, weight, 0.0)
        return carry

    lax.fori_loop(0, ns // 2, slots, 0)

    for has, copies in ((has_down, up), (has_up, down)):
        @pl.when(has)
        def _(copies=copies):
            for copy in copies[:3]:
                copy.wait_recv()

        @pl.when(jnp.logical_and(has, is_last))
        def _(copies=copies):
            copies[3].wait_recv()

    for side in range(2):
        for k, count, at in ((3, 3, 0), (2, 2, 3), (1, 1, 5)):
            row = EDGE - count if side == 0 else EDGE + ROWS
            push[k, :, :, pl.ds(row, count), :] = force_in[side, :, :, pl.ds(at, count), :]

    for j in range(1, STEPS + 1):
        edges(free.at[j - 1], None, free.at[j], j)

    for piece in range(PIECES):
        tile = []
        for f in range(FIELDS):
            x = free[STEPS, f, :, pl.ds(EDGE + piece * PIECE, PIECE), :]
            top = jnp.max(jnp.abs(x), axis=(0, 1, 2), keepdims=True)
            safe = jnp.maximum(top, 1e-30)
            y = jnp.round(x * (LEVELS / safe))
            coded[f, :, pl.ds(piece * PIECE, PIECE), :] = y.astype(jnp.int32).astype(jnp.int16)
            tile.append(jnp.broadcast_to(safe[0] * (1.0 / LEVELS), (1, LANES)))
        tile += [jnp.zeros((1, LANES), f32)] * (8 - FIELDS)
        coded_scale[piece] = jnp.concatenate(tile, axis=0)

    def z_copy(src, dst, i):
        return pltpu.make_async_remote_copy(
            src_ref=src, dst_ref=dst, send_sem=z_send.at[i], recv_sem=z_recv.at[i],
            device_id=(t - 1, s), device_id_type=MESH,
        )

    z_copies = [z_copy(coded_scale, got_scale, 0), z_copy(coded, got, 1)]

    @pl.when(has_earlier)
    def _():
        for copy in z_copies:
            copy.start()

    @pl.when(has_later)
    def _():
        for row, count, at in ((EDGE - 3, 3, 0), (EDGE + ROWS, 3, 0)):
            forced[1, :, :, pl.ds(row, count), :] = push[3, :, :, pl.ds(row, count), :]

    @pl.when(is_last)
    def _():
        edges(forced.at[0], push.at[3], forced.at[1], 1)

    for j in range(2, STEPS + 1):
        edges(forced.at[j - 1], push.at[STEPS - j], forced.at[j], j)

    for part, ref in enumerate((forced, free)):
        for k in range(STEPS):
            value = jnp.concatenate([ref[STEPS - k, 4, b, own, :] for b in range(BLOCKS)], axis=1)
            high = value.astype(bf16)
            at = 2 * (part * STEPS + k) * ROWS
            energy[pl.ds(at, ROWS), :] = high
            energy[pl.ds(at + ROWS, ROWS), :] = (value - high.astype(f32)).astype(bf16)

    def pick(p, carry):
        out = jnp.dot(energy[...], column[p], preferred_element_type=f32)
        weight = row_area[p]
        for k in range(SETS):
            at = 2 * k * ROWS
            both = (out[at : at + ROWS] + out[at + ROWS : at + 2 * ROWS]) * weight
            line = jnp.sum(both, axis=0, keepdims=True)
            for half in range(2):
                picked[k, pl.ds(2 * p + half, 1), :] = line[:, half * LANES : (half + 1) * LANES]
        return carry

    lax.fori_loop(0, ns // 2, pick, 0, unroll=4 if ns >= 8 else 1)
    ids = acts[...]
    wide = jnp.bitwise_and(lax.broadcasted_iota(jnp.int32, ids.shape, 1), 2 * GROUP - 1)
    total = jnp.zeros(ids.shape, f32)
    for k in range(SETS):
        values = picked[k]
        for a in range(ACT):
            part = jnp.sum(jnp.where(ids == a, values, 0.0), axis=1, keepdims=True)
            total = jnp.where(wide == k * ACT + a, part, total)
    partial[...] = total.reshape(partial.shape)

    pl.semaphore_wait(greet_y, len(same_x))
    to_owner = []
    for i, o in enumerate(around):
        dev = beside(o)
        to_owner.append(pltpu.make_async_remote_copy(
            src_ref=partial.at[dev[1]], dst_ref=mine.at[inverse(o)],
            send_sem=a_send.at[i], recv_sem=a_recv.at[inverse(o)],
            device_id=dev, device_id_type=MESH,
        ))
    for copy in to_owner:
        copy.start()
    mine[ns - 1] = partial[s]

    rate = jnp.zeros((1, LANES), f32)
    for a in range(ACT):
        rate = jnp.where(lax.rem(lane1, ACT) == a, rate_ref[a], rate)
    k_of = lax.rem(lane1, GROUP) // ACT
    k_f = k_of.astype(f32)
    q_of = lane1 // GROUP
    decay = [jnp.exp(-float(m) * rate) for m in range(STEPS)]
    later_weight[0] = jnp.zeros((1, LANES), f32)
    for j in range(1, nt):
        forced_part = jnp.exp(-float(STEPS * (j - 1)) * rate)
        start_part = jnp.exp(-float(STEPS * (j - 2)) * rate) if j > 1 else 0.0
        row = jnp.where(q_of == 0, forced_part, 0.0) + jnp.where(q_of == 1, start_part, 0.0)
        if j == 1:
            row = row + jnp.where(q_of == 5, 1.0, 0.0)
        later_weight[j] = row
    pl.semaphore_wait(greet_farther, len(farther))
    for i, o in enumerate(around):
        pltpu.make_async_remote_copy(
            src_ref=partial.at[s], dst_ref=mine.at[i], send_sem=a_send.at[i], recv_sem=a_recv.at[i],
            device_id=beside(o), device_id_type=MESH,
        ).wait_recv()
    loads = jnp.sum(mine[...], axis=0)
    summed = loads * jnp.exp(-k_f * rate)
    for shift, low in ((8, k_of < 2), (4, lax.rem(k_of, 2) == 0)):
        other = jnp.where(low, pltpu.roll(summed, LANES - shift, 1), pltpu.roll(summed, shift, 1))
        summed = summed + other
    send[...] = jnp.where(q_of < 4, summed, loads)

    to_earlier = {
        j: pltpu.make_async_remote_copy(
            src_ref=send, dst_ref=later.at[j], send_sem=t_send.at[j], recv_sem=t_recv.at[j],
            device_id=(t - j, s), device_id_type=MESH,
        )
        for j in time_offsets(nt)
    }
    for j, copy in to_earlier.items():
        pl.when(t >= j)(copy.start)

    @pl.when(has_later)
    def _():
        for copy in z_copies:
            copy.wait_recv()

    @pl.when(is_last)
    def _():
        got[...] = jnp.zeros(got.shape, jnp.int16)
        got_scale[...] = jnp.zeros(got_scale.shape, f32)

    for piece in range(PIECES):
        rows = pl.ds(piece * PIECE, PIECE)
        for f in range(FIELDS):
            factor = got_scale[piece, f : f + 1, :]
            for b in range(BLOCKS):
                value = got[f, b, rows, :].astype(jnp.int32).astype(f32) * factor
                points[0, f, rows, pl.ds(b * LANES, LANES)] = (
                    value + forced[STEPS, f, b, pl.ds(EDGE + piece * PIECE, PIECE), :]
                )

    for j, copy in to_earlier.items():
        pl.when(t + j < nt)(copy.wait_recv)
    arrived = jnp.sum(later[...] * later_weight[...], axis=0)
    loads = loads + pltpu.roll(arrived, LANES - 5 * GROUP, 1)
    incoming = arrived + pltpu.roll(arrived, LANES - GROUP, 1)
    result = loads + jnp.exp(-(STEPS - k_f) * rate) * incoming
    for m in range(1, STEPS):
        moved = pltpu.roll(loads, LANES - ACT * m, 1)
        result = result + jnp.where(k_of + m < STEPS, decay[m] * moved, 0.0)
    for k in range(STEPS):
        moved = pltpu.roll(result, LANES - ACT * k, 1) if k else result
        states[0, pl.ds(k, 1), :] = moved[:, :ACT]

    for j, copy in to_earlier.items():
        pl.when(t >= j)(copy.wait_send)
    for copy in to_owner:
        copy.wait_send()
    for has, copies in ((has_up, up), (has_down, down)):
        @pl.when(has)
        def _(copies=copies):
            for copy in copies[:3]:
                copy.wait_send()

        @pl.when(jnp.logical_and(has, is_last))
        def _(copies=copies):
            copies[3].wait_send()

    @pl.when(has_earlier)
    def _():
        for copy in z_copies:
            copy.wait_send()


def per_device(
    c_points, terminal, forcing, conductance, coupling, flap_cells, flap_actuator, flap_area, actuator_rate
):
    nt, ns = lax.axis_size("tm"), lax.axis_size("space")
    anywhere = pl.BlockSpec(memory_space=pl.ANY)
    vmem = pl.BlockSpec(memory_space=pltpu.VMEM)
    smem = pl.BlockSpec(memory_space=pltpu.SMEM)
    dma = pltpu.SemaphoreType.DMA
    regular = pltpu.SemaphoreType.REGULAR
    i32 = jnp.int32
    block = (FIELDS, BLOCKS, EXT, LANES)
    points, states = pl.pallas_call(
        whole,
        out_shape=(
            jax.ShapeDtypeStruct((1, FIELDS, ROWS, COLS), f32),
            jax.ShapeDtypeStruct((1, STEPS, ACT), f32),
        ),
        in_specs=[anywhere] * 4 + [smem] + [anywhere] * 3 + [smem],
        out_specs=(vmem, vmem),
        scratch_shapes=[
            pltpu.VMEM((STEPS + 1,) + block, f32),
            pltpu.VMEM((STEPS + 1,) + block, f32),
            pltpu.VMEM((STEPS,) + block, f32),
            pltpu.VMEM(block[1:], f32),
            pltpu.VMEM((STEPS, FIELDS, ROWS, COLS), bf16),
            pltpu.VMEM((2, FIELDS, BLOCKS, 8, LANES), f32),
            pltpu.VMEM((2, FIELDS, BLOCKS, 8, LANES), f32),
            pltpu.VMEM((ns, LANES), i32),
            pltpu.VMEM((ns, LANES), i32),
            pltpu.VMEM((ns, LANES), f32),
            pltpu.VMEM((FIELDS, BLOCKS, ROWS, LANES), jnp.int16),
            pltpu.VMEM((PIECES, 8, LANES), f32),
            pltpu.VMEM((FIELDS, BLOCKS, ROWS, LANES), jnp.int16),
            pltpu.VMEM((PIECES, 8, LANES), f32),
            pltpu.VMEM((ns // 2, COLS, 2 * LANES), bf16),
            pltpu.VMEM((ns // 2, ROWS, 2 * LANES), f32),
            pltpu.VMEM((2 * SETS * ROWS, COLS), bf16),
            pltpu.VMEM((SETS, ns, LANES), f32),
            pltpu.VMEM((ns, 1, LANES), f32),
            pltpu.VMEM((ns, 1, LANES), f32),
            pltpu.VMEM((nt, 1, LANES), f32),
            pltpu.VMEM((nt, 1, LANES), f32),
            pltpu.VMEM((1, LANES), f32),
            dma((16,)), dma((2,)), dma((2,)), dma((8,)), dma((8,)),
            dma((ns,)), dma((ns,)), dma((nt,)), dma((nt,)),
            regular, regular, regular,
        ],
        compiler_params=pltpu.CompilerParams(
            collective_id=0, has_side_effects=True, vmem_limit_bytes=58 * 2**20
        ),
        name="whole",
    )(c_points, terminal, forcing, conductance, coupling, flap_cells, flap_actuator, flap_area, actuator_rate)
    return (points, states)


def solution(mesh):
    placed = (
        P("tm", None, "space", None),
        P(None, "space", None),
        P("tm", None, None, "space", None),
        P("space", None),
        P(),
        P("space", None),
        P("space", None),
        P("space", None),
        P("space"),
    )
    return jax.shard_map(
        per_device,
        mesh=mesh,
        in_specs=placed,
        out_specs=(P("tm", None, "space", None), P("tm", None, "space")),
        check_vma=False,
    )
```

```python
import jax
import jax.numpy as jnp
from jax import lax
from jax.experimental import pallas as pl
from jax.experimental.pallas import tpu as pltpu
from jax.sharding import PartitionSpec as P

STEPS = 4
ACT = 4
FIELDS = 5
ROWS = 64
COLS = 512
LANES = 128
BLOCKS = COLS // LANES
EDGE = 16
EXT = ROWS + 2 * EDGE
PIECE = 16
PIECES = ROWS // PIECE
GROUP = STEPS * ACT
SETS = 2 * STEPS
RIM = 4
INNER = ROWS - 2 * RIM
MESH = pl.DeviceIdType.MESH
LEVELS = 32767.0
f32 = jnp.float32
bf16 = jnp.bfloat16


def pair(ref, f, b, rows, shift):
    return jnp.concatenate([ref[f, b, pl.ds(row + shift, 8), :] for row in rows], axis=0)


def step_map(src, cond, rows, coupling, lane):
    first, last = lane == 0, lane == LANES - 1
    none = jnp.zeros(lane.shape, bf16)
    left, right = {}, {}
    for f in range(FIELDS):
        for b in range(BLOCKS):
            short = pair(src, f, b, rows, 0).astype(bf16)
            left[f, b] = pltpu.roll(short, 1, 1)
            right[f, b] = pltpu.roll(short, LANES - 1, 1)
    result = [[None] * BLOCKS for _ in range(FIELDS)]
    for b in range(BLOCKS):
        weight = jnp.concatenate([cond[b, pl.ds(row, 8), :] for row in rows], axis=0)
        keep, from_north, from_south, from_side = 1.0 - weight, 0.35 * weight, 0.15 * weight, 0.1 * weight
        mixed = []
        for f in range(FIELDS):
            west = jnp.where(first, left[f, b - 1] if b else none, left[f, b])
            east = jnp.where(last, right[f, b + 1] if b < BLOCKS - 1 else none, right[f, b])
            side = (jnp.bfloat16(3.0) * west + jnp.bfloat16(2.0) * east).astype(f32)
            mixed.append(
                keep * pair(src, f, b, rows, 0) + from_north * pair(src, f, b, rows, -1)
                + from_south * pair(src, f, b, rows, 1) + from_side * side
            )
        for f in range(FIELDS):
            total = coupling[0][f] * mixed[0]
            for g in range(1, FIELDS):
                total = total + coupling[g][f] * mixed[g]
            result[f][b] = total
    return result


def space_offsets(ns):
    nc = 2
    nx = min(4, ns // nc)
    ny = ns // (nc * nx)
    far = lambda d, n: min(d, n - d)
    steps = [(y, x, c) for y in range(ny) for x in range(nx) for c in range(nc)][1:]
    steps.sort(key=lambda o: -(2 * far(o[0], ny) + 2 * far(o[1], nx) + o[2]))
    return steps, (ny, nx, nc)


def time_offsets(nt):
    return sorted(range(1, nt), key=lambda j: -min(j, nt - j))


def offsets(distances, n):
    return sorted({d % n for d in distances} - {0})


def whole(
    points_in, terminal, forcing, conductance, coupling_ref, cells_in, acts_in, area_in, rate_ref,
    points, states,
    free, forced, push, cond, force_own, force_out, force_in, cells, acts, area,
    coded, coded_scale, got, got_scale,
    column, row_inner, row_rim, inner, rim, picked, picked_rim, partial, mine, later, later_weight, send, result_rows,
    in_sem, z_send, z_recv, s_send, s_recv, a_send, a_recv, t_send, t_recv,
    greet_y, greet_far, greet_farther,
):
    nt, ns = lax.axis_size("tm"), lax.axis_size("space")
    t, s = lax.axis_index("tm"), lax.axis_index("space")
    around, (ny, nx, nc) = space_offsets(ns)
    place = (s // (nx * nc), lax.rem(s // nc, nx), lax.rem(s, nc))
    has_up, has_down = s < ns - 1, s > 0
    has_later, has_earlier = t < nt - 1, t > 0
    is_last = jnp.logical_not(has_later)

    def beside(o):
        y, x = lax.rem(place[0] + o[0], ny), lax.rem(place[1] + o[1], nx)
        c = 1 - place[2] if o[2] else place[2]
        return (t, (y * nx + x) * nc + c)

    def inverse(o):
        return around.index(((-o[0]) % ny, (-o[1]) % nx, o[2]))

    def in_time(j):
        return (lax.rem(t + j, nt), s)

    def signal(sem, dev):
        pl.semaphore_signal(sem, inc=1, device_id=dev, device_id_type=MESH)

    own = pl.ds(EDGE, ROWS)

    def load(src, dst, i):
        return pltpu.make_async_copy(src, dst, in_sem.at[i])

    def columns(src, dst, i):
        return [
            load(
                src.at[..., pl.ds(b * LANES, LANES)],
                dst.at[:, b, own, :] if len(dst.shape) == 4 else dst.at[b, own, :], i + b,
            )
            for b in range(BLOCKS)
        ]

    first_loads = columns(points_in.at[0], free.at[0], 0) + columns(conductance, cond, 4)
    force_load = load(forcing.at[0], force_own, 8)
    slot_loads = [load(cells_in, cells, 9), load(acts_in, acts, 10), load(area_in, area, 11)]
    end_loads = columns(terminal, forced.at[0], 12)
    for copy in slot_loads + [force_load] + first_loads[BLOCKS:] + first_loads[:BLOCKS]:
        copy.start()

    @pl.when(is_last)
    def _():
        for copy in end_loads:
            copy.start()

    later[...] = jnp.zeros(later.shape, f32)
    barrier = pltpu.get_barrier_semaphore()
    near_time = offsets((1, -1, 2, -2), nt)
    near_space = [o for o in around if o[0] == 0 or o[1:] == (0, 0)]
    for j in near_time:
        signal(barrier, in_time(j))
    signal(barrier, (t, lax.rem(s + 1, ns)))
    signal(barrier, (t, lax.rem(s + ns - 1, ns)))
    for o in near_space:
        signal(barrier, beside(o))

    lane16 = lax.broadcasted_iota(jnp.int32, (16, LANES), 1)
    lane1 = lax.broadcasted_iota(jnp.int32, (1, LANES), 1)
    coupling = [[coupling_ref[g, f] for f in range(FIELDS)] for g in range(FIELDS)]

    def advance(src, add, dst, rows):
        value = step_map(src, cond, rows, coupling, lane16)
        for f in range(FIELDS):
            for b in range(BLOCKS):
                for half, row in enumerate(rows):
                    part = value[f][b][8 * half : 8 * half + 8]
                    if add is not None:
                        part = part + add[f, b, pl.ds(row, 8), :]
                    dst[f, b, pl.ds(row, 8), :] = part

    def interior(src, add, dst, j, beside=None):
        def body(i, carry):
            for tile in (2 * i, 2 * i + 1):
                if beside is not None:
                    beside(tile)
                row = jnp.minimum(EDGE + j + 16 * tile, EDGE + ROWS - j - 16)
                advance(src, add, dst, (row, row + 8))
            return carry

        lax.fori_loop(0, ROWS // 32, body, 0)

    def edges(src, add, dst, j):
        advance(src, add, dst, (EDGE - 4 + j, EDGE + ROWS - 4 - j))

    for copy in slot_loads:
        copy.wait()

    numbers = lax.broadcasted_iota(jnp.int32, (COLS, LANES), 0).astype(jnp.int16)
    one, zero = jnp.ones((16, LANES), bf16), jnp.zeros((16, LANES), bf16)

    def slots(p, carry):
        for half in range(2):
            cell = cells[pl.ds(2 * p + half, 1), :]
            lanes = pl.ds(half * LANES, LANES)
            col = jnp.broadcast_to(jnp.bitwise_and(cell, COLS - 1), (16, LANES)).astype(jnp.int16)
            for at in range(0, COLS, 16):
                column[p, pl.ds(at, 16), lanes] = jnp.where(col == numbers[at : at + 16], one, zero)
            row = jnp.broadcast_to(lax.shift_right_arithmetic(cell, 9), (INNER, LANES))
            weight = jnp.broadcast_to(area[pl.ds(2 * p + half, 1), :], (INNER, LANES))
            at = lax.broadcasted_iota(jnp.int32, (INNER, LANES), 0) + RIM
            row_inner[p, :, lanes] = jnp.where(row == at, weight, 0.0)
            at = lax.broadcasted_iota(jnp.int32, (2 * RIM, LANES), 0)
            at = jnp.where(at < RIM, at, at + INNER)
            row_rim[p, :, lanes] = jnp.where(row[: 2 * RIM] == at, weight[: 2 * RIM], 0.0)
        return carry

    lax.fori_loop(0, ns // 2, slots, 0)


    force_load.wait()
    for side, at in ((0, 13), (1, 0)):
        for f in range(FIELDS):
            for k, count, to in ((3, 3, 0), (2, 2, 3), (1, 1, 5)):
                near = force_own[k, f, pl.ds(ROWS - 16 if side == 0 else 0, 16), :].astype(f32)
                near = near[16 - count :] if side == 0 else near[:count]
                for b in range(BLOCKS):
                    force_out[side, f, b, pl.ds(to, count), :] = near[:, b * LANES : (b + 1) * LANES]
            for b in range(BLOCKS):
                force_out[side, f, b, pl.ds(6, 2), :] = jnp.zeros((2, LANES), f32)

    @pl.when(jnp.logical_not(has_down))
    def _():
        free[0, :, :, pl.ds(8, 8), :] = jnp.zeros((FIELDS, BLOCKS, 8, LANES), f32)
        forced[0, :, :, pl.ds(8, 8), :] = jnp.zeros((FIELDS, BLOCKS, 8, LANES), f32)
        cond[:, pl.ds(8, 8), :] = jnp.zeros((BLOCKS, 8, LANES), f32)
        force_in[0] = jnp.zeros((FIELDS, BLOCKS, 8, LANES), f32)

    @pl.when(jnp.logical_not(has_up))
    def _():
        high = pl.ds(EDGE + ROWS, 8)
        free[0, :, :, high, :] = jnp.zeros((FIELDS, BLOCKS, 8, LANES), f32)
        forced[0, :, :, high, :] = jnp.zeros((FIELDS, BLOCKS, 8, LANES), f32)
        cond[:, high, :] = jnp.zeros((BLOCKS, 8, LANES), f32)
        force_in[1] = jnp.zeros((FIELDS, BLOCKS, 8, LANES), f32)

    def widen(i, carry):
        k, f = i // FIELDS, lax.rem(i, FIELDS)
        value = force_own[k, f].astype(f32)
        for b in range(BLOCKS):
            push[k, f, b, own, :] = value[:, b * LANES : (b + 1) * LANES]
        return carry

    lax.fori_loop(0, STEPS * FIELDS, widen, 0)

    for copy in first_loads[BLOCKS:]:
        copy.wait()

    @pl.when(is_last)
    def _():
        for copy in end_loads:
            copy.wait()

    @pl.when(has_later)
    def _():
        forced[1, :, :, own, :] = push[3, :, :, own, :]

    @pl.when(is_last)
    def _():
        interior(forced.at[0], push.at[3], forced.at[1], 1)

    for j in range(2, STEPS):
        interior(forced.at[j - 1], push.at[STEPS - j], forced.at[j], j)

    for copy in first_loads[:BLOCKS]:
        copy.wait()
    pl.semaphore_wait(barrier, len(near_time) + 2 + len(near_space))

    def s_copy(src, dst, i, to):
        return pltpu.make_async_remote_copy(
            src_ref=src, dst_ref=dst, send_sem=s_send.at[i], recv_sem=s_recv.at[i],
            device_id=(t, to), device_id_type=MESH,
        )

    def halo(side):
        to = s + 1 if side == 0 else s - 1
        mine_rows = pl.ds(EDGE + ROWS - 8 if side == 0 else EDGE, 8)
        their_rows = pl.ds(8 if side == 0 else EDGE + ROWS, 8)
        i = 4 * side
        return [
            s_copy(free.at[0, :, :, mine_rows, :], free.at[0, :, :, their_rows, :], i, to),
            s_copy(cond.at[:, mine_rows, :], cond.at[:, their_rows, :], i + 1, to),
            s_copy(force_out.at[side], force_in.at[side], i + 2, to),
            s_copy(forced.at[0, :, :, mine_rows, :], forced.at[0, :, :, their_rows, :], i + 3, to),
        ]

    up, down = halo(0), halo(1)
    for has, copies in ((has_up, up), (has_down, down)):
        @pl.when(has)
        def _(copies=copies):
            for copy in copies[:3]:
                copy.start()

        @pl.when(jnp.logical_and(has, is_last))
        def _(copies=copies):
            copies[3].start()

    same_x = [o for o in near_space if o[1:] == (0, 0)]
    for o in same_x:
        signal(greet_y, beside(o))
    far = offsets((2, -2), nt)
    for j in far:
        signal(greet_far, in_time(j))

    parts = (forced, free)

    def two_terms(value):
        high = value.astype(bf16).astype(f32)
        return jnp.concatenate([high, value - high], axis=0).astype(bf16)

    def fill_inner(part):
        for k in range(STEPS):
            value = jnp.concatenate(
                [parts[part][STEPS - k, 4, b, pl.ds(EDGE + RIM, INNER), :] for b in range(BLOCKS)], axis=1
            )
            inner[pl.ds(2 * INNER * (part * STEPS + k), 2 * INNER), :] = two_terms(value)

    def pick(p, terms, first, sets, rows, weight, to):
        out = jnp.dot(
            terms[pl.ds(2 * rows * first, 2 * rows * sets), :], column[p], preferred_element_type=f32
        )
        for k in range(sets):
            at = 2 * k * rows
            both = (out[at : at + rows] + out[at + rows : at + 2 * rows]) * weight[p]
            line = jnp.sum(both, axis=0, keepdims=True)
            for half in range(2):
                to[first + k, pl.ds(2 * p + half, 1), :] = line[:, half * LANES : (half + 1) * LANES]

    def pick_inner(part, p):
        pick(p, inner, part * STEPS, STEPS, INNER, row_inner, picked)

    interior(forced.at[STEPS - 1], push.at[0], forced.at[STEPS], STEPS)
    fill_inner(0)
    pairs = ns // 2
    tiles = ROWS // 16
    shared = pairs >= STEPS * tiles
    for j in range(1, STEPS + 1):
        def some(i, j=j):
            if shared:
                pick_inner(0, (j - 1) * tiles + i)

        interior(free.at[j - 1], None, free.at[j], j, some)
    for p in range(STEPS * tiles if shared else 0, pairs):
        pick_inner(0, p)
    fill_inner(1)

    pl.semaphore_wait(greet_far, len(far))
    farther = offsets((4, -4), nt)
    for j in farther:
        signal(greet_farther, in_time(j))

    for has, copies in ((has_down, up), (has_up, down)):
        @pl.when(has)
        def _(copies=copies):
            for copy in copies[:3]:
                copy.wait_recv()

        @pl.when(jnp.logical_and(has, is_last))
        def _(copies=copies):
            copies[3].wait_recv()

    for side in range(2):
        for k, count, at in ((3, 3, 0), (2, 2, 3), (1, 1, 5)):
            row = EDGE - count if side == 0 else EDGE + ROWS
            push[k, :, :, pl.ds(row, count), :] = force_in[side, :, :, pl.ds(at, count), :]

    todo = [0]

    def some_free():
        todo[0] += 1
        for p in range((todo[0] - 1) * pairs // 7, todo[0] * pairs // 7):
            pick_inner(1, p)

    for j in range(1, STEPS + 1):
        some_free()
        edges(free.at[j - 1], None, free.at[j], j)

    for piece in range(PIECES):
        tile = []
        for f in range(FIELDS):
            x = free[STEPS, f, :, pl.ds(EDGE + piece * PIECE, PIECE), :]
            top = jnp.max(jnp.abs(x), axis=(0, 1, 2), keepdims=True)
            safe = jnp.maximum(top, 1e-30)
            y = jnp.round(x * (LEVELS / safe))
            coded[f, :, pl.ds(piece * PIECE, PIECE), :] = y.astype(jnp.int32).astype(jnp.int16)
            tile.append(jnp.broadcast_to(safe[0] * (1.0 / LEVELS), (1, LANES)))
        tile += [jnp.zeros((1, LANES), f32)] * (8 - FIELDS)
        coded_scale[piece] = jnp.concatenate(tile, axis=0)

    def z_copy(src, dst, i):
        return pltpu.make_async_remote_copy(
            src_ref=src, dst_ref=dst, send_sem=z_send.at[i], recv_sem=z_recv.at[i],
            device_id=(t - 1, s), device_id_type=MESH,
        )

    z_copies = [z_copy(coded_scale, got_scale, 0), z_copy(coded, got, 1)]

    @pl.when(has_earlier)
    def _():
        for copy in z_copies:
            copy.start()

    @pl.when(has_later)
    def _():
        for row, count, at in ((EDGE - 3, 3, 0), (EDGE + ROWS, 3, 0)):
            forced[1, :, :, pl.ds(row, count), :] = push[3, :, :, pl.ds(row, count), :]

    @pl.when(is_last)
    def _():
        edges(forced.at[0], push.at[3], forced.at[1], 1)

    for j in range(2, STEPS + 1):
        some_free()
        edges(forced.at[j - 1], push.at[STEPS - j], forced.at[j], j)

    for part, ref in enumerate(parts):
        for k in range(STEPS):
            value = jnp.concatenate(
                [
                    jnp.concatenate(
                        [ref[STEPS - k, 4, b, pl.ds(EDGE, RIM), :],
                         ref[STEPS - k, 4, b, pl.ds(EDGE + ROWS - RIM, RIM), :]], axis=0
                    )
                    for b in range(BLOCKS)
                ],
                axis=1,
            )
            rim[pl.ds(4 * RIM * (part * STEPS + k), 4 * RIM), :] = two_terms(value)

    def pick_rim(p, carry):
        pick(p, rim, 0, SETS, 2 * RIM, row_rim, picked_rim)
        return carry

    lax.fori_loop(0, pairs, pick_rim, 0, unroll=8 if pairs >= 8 else 1)
    ids = acts[...]
    wide = jnp.bitwise_and(lax.broadcasted_iota(jnp.int32, ids.shape, 1), 2 * GROUP - 1)
    total = jnp.zeros(ids.shape, f32)
    for k in range(SETS):
        values = picked[k] + picked_rim[k]
        for a in range(ACT):
            part = jnp.sum(jnp.where(ids == a, values, 0.0), axis=1, keepdims=True)
            total = jnp.where(wide == k * ACT + a, part, total)
    partial[...] = total.reshape(partial.shape)

    pl.semaphore_wait(greet_y, len(same_x))
    to_owner = []
    for i, o in enumerate(around):
        dev = beside(o)
        to_owner.append(pltpu.make_async_remote_copy(
            src_ref=partial.at[dev[1]], dst_ref=mine.at[inverse(o)],
            send_sem=a_send.at[i], recv_sem=a_recv.at[inverse(o)],
            device_id=dev, device_id_type=MESH,
        ))
    for copy in to_owner:
        copy.start()
    mine[ns - 1] = partial[s]

    rate = jnp.zeros((1, LANES), f32)
    for a in range(ACT):
        rate = jnp.where(lax.rem(lane1, ACT) == a, rate_ref[a], rate)
    k_of = lax.rem(lane1, GROUP) // ACT
    k_f = k_of.astype(f32)
    q_of = lane1 // GROUP
    decay = [jnp.exp(-float(m) * rate) for m in range(STEPS)]
    later_weight[0] = jnp.zeros((1, LANES), f32)
    for j in range(1, nt):
        forced_part = jnp.exp(-float(STEPS * (j - 1)) * rate)
        start_part = jnp.exp(-float(STEPS * (j - 2)) * rate) if j > 1 else 0.0
        row = jnp.where(q_of == 0, forced_part, 0.0) + jnp.where(q_of == 1, start_part, 0.0)
        if j == 1:
            row = row + jnp.where(q_of == 5, 1.0, 0.0)
        later_weight[j] = row
    pl.semaphore_wait(greet_farther, len(farther))
    for i, o in enumerate(around):
        pltpu.make_async_remote_copy(
            src_ref=partial.at[s], dst_ref=mine.at[i], send_sem=a_send.at[i], recv_sem=a_recv.at[i],
            device_id=beside(o), device_id_type=MESH,
        ).wait_recv()
    loads = jnp.sum(mine[...], axis=0)
    summed = loads * jnp.exp(-k_f * rate)
    for shift, low in ((8, k_of < 2), (4, lax.rem(k_of, 2) == 0)):
        other = jnp.where(low, pltpu.roll(summed, LANES - shift, 1), pltpu.roll(summed, shift, 1))
        summed = summed + other
    send[...] = jnp.where(q_of < 4, summed, loads)

    to_earlier = {
        j: pltpu.make_async_remote_copy(
            src_ref=send, dst_ref=later.at[j], send_sem=t_send.at[j], recv_sem=t_recv.at[j],
            device_id=(t - j, s), device_id_type=MESH,
        )
        for j in time_offsets(nt)
    }
    for j, copy in to_earlier.items():
        pl.when(t >= j)(copy.start)

    @pl.when(has_later)
    def _():
        for copy in z_copies:
            copy.wait_recv()

    @pl.when(is_last)
    def _():
        got[...] = jnp.zeros(got.shape, jnp.int16)
        got_scale[...] = jnp.zeros(got_scale.shape, f32)

    for piece in range(PIECES):
        rows = pl.ds(piece * PIECE, PIECE)
        for f in range(FIELDS):
            factor = got_scale[piece, f : f + 1, :]
            for b in range(BLOCKS):
                value = got[f, b, rows, :].astype(jnp.int32).astype(f32) * factor
                result_rows[f, rows, pl.ds(b * LANES, LANES)] = (
                    value + forced[STEPS, f, b, pl.ds(EDGE + piece * PIECE, PIECE), :]
                )

    store = load(result_rows, points.at[0], 8)
    store.start()
    for j, copy in to_earlier.items():
        pl.when(t + j < nt)(copy.wait_recv)
    arrived = jnp.sum(later[...] * later_weight[...], axis=0)
    loads = loads + pltpu.roll(arrived, LANES - 5 * GROUP, 1)
    incoming = arrived + pltpu.roll(arrived, LANES - GROUP, 1)
    result = loads + jnp.exp(-(STEPS - k_f) * rate) * incoming
    for m in range(1, STEPS):
        moved = pltpu.roll(loads, LANES - ACT * m, 1)
        result = result + jnp.where(k_of + m < STEPS, decay[m] * moved, 0.0)
    for k in range(STEPS):
        moved = pltpu.roll(result, LANES - ACT * k, 1) if k else result
        states[0, pl.ds(k, 1), :] = moved[:, :ACT]

    store.wait()
    for j, copy in to_earlier.items():
        pl.when(t >= j)(copy.wait_send)
    for copy in to_owner:
        copy.wait_send()
    for has, copies in ((has_up, up), (has_down, down)):
        @pl.when(has)
        def _(copies=copies):
            for copy in copies[:3]:
                copy.wait_send()

        @pl.when(jnp.logical_and(has, is_last))
        def _(copies=copies):
            copies[3].wait_send()

    @pl.when(has_earlier)
    def _():
        for copy in z_copies:
            copy.wait_send()


def hand_over(points_in, states_in, points, states, rows, small, sem):
    into = [
        pltpu.make_async_copy(points_in.at[0, f], rows.at[f], sem.at[0, f]) for f in range(FIELDS)
    ] + [pltpu.make_async_copy(states_in, small, sem.at[0, FIELDS])]
    out = [
        pltpu.make_async_copy(rows.at[f], points.at[0, f], sem.at[1, f]) for f in range(FIELDS)
    ] + [pltpu.make_async_copy(small, states, sem.at[1, FIELDS])]
    for copy in into:
        copy.start()
    for first, then in zip(into, out):
        first.wait()
        then.start()
    for copy in out:
        copy.wait()


def per_device(
    c_points, terminal, forcing, conductance, coupling, flap_cells, flap_actuator, flap_area, actuator_rate
):
    nt, ns = lax.axis_size("tm"), lax.axis_size("space")
    anywhere = pl.BlockSpec(memory_space=pl.ANY)
    vmem = pl.BlockSpec(memory_space=pltpu.VMEM)
    smem = pl.BlockSpec(memory_space=pltpu.SMEM)
    dma = pltpu.SemaphoreType.DMA
    regular = pltpu.SemaphoreType.REGULAR
    i32 = jnp.int32
    block = (FIELDS, BLOCKS, EXT, LANES)
    points, states = pl.pallas_call(
        whole,
        out_shape=(
            jax.ShapeDtypeStruct((1, FIELDS, ROWS, COLS), f32),
            jax.ShapeDtypeStruct((1, STEPS, ACT), f32),
        ),
        in_specs=[anywhere] * 4 + [smem] + [anywhere] * 3 + [smem],
        out_specs=(anywhere, vmem),
        scratch_shapes=[
            pltpu.VMEM((STEPS + 1,) + block, f32),
            pltpu.VMEM((STEPS + 1,) + block, f32),
            pltpu.VMEM((STEPS,) + block, f32),
            pltpu.VMEM(block[1:], f32),
            pltpu.VMEM((STEPS, FIELDS, ROWS, COLS), bf16),
            pltpu.VMEM((2, FIELDS, BLOCKS, 8, LANES), f32),
            pltpu.VMEM((2, FIELDS, BLOCKS, 8, LANES), f32),
            pltpu.VMEM((ns, LANES), i32),
            pltpu.VMEM((ns, LANES), i32),
            pltpu.VMEM((ns, LANES), f32),
            pltpu.VMEM((FIELDS, BLOCKS, ROWS, LANES), jnp.int16),
            pltpu.VMEM((PIECES, 8, LANES), f32),
            pltpu.VMEM((FIELDS, BLOCKS, ROWS, LANES), jnp.int16),
            pltpu.VMEM((PIECES, 8, LANES), f32),
            pltpu.VMEM((ns // 2, COLS, 2 * LANES), bf16),
            pltpu.VMEM((ns // 2, INNER, 2 * LANES), f32),
            pltpu.VMEM((ns // 2, 2 * RIM, 2 * LANES), f32),
            pltpu.VMEM((2 * SETS * INNER, COLS), bf16),
            pltpu.VMEM((4 * SETS * RIM, COLS), bf16),
            pltpu.VMEM((SETS, ns, LANES), f32),
            pltpu.VMEM((SETS, ns, LANES), f32),
            pltpu.VMEM((ns, 1, LANES), f32),
            pltpu.VMEM((ns, 1, LANES), f32),
            pltpu.VMEM((nt, 1, LANES), f32),
            pltpu.VMEM((nt, 1, LANES), f32),
            pltpu.VMEM((1, LANES), f32),
            pltpu.VMEM((FIELDS, ROWS, COLS), f32),
            dma((16,)), dma((2,)), dma((2,)), dma((8,)), dma((8,)),
            dma((ns,)), dma((ns,)), dma((nt,)), dma((nt,)),
            regular, regular, regular,
        ],
        compiler_params=pltpu.CompilerParams(
            collective_id=0, has_side_effects=True, vmem_limit_bytes=58 * 2**20
        ),
        name="whole",
    )(c_points, terminal, forcing, conductance, coupling, flap_cells, flap_actuator, flap_area, actuator_rate)
    return pl.pallas_call(
        hand_over,
        out_shape=(
            jax.ShapeDtypeStruct(points.shape, f32),
            jax.ShapeDtypeStruct(states.shape, f32),
        ),
        in_specs=[anywhere] * 2,
        out_specs=(anywhere,) * 2,
        scratch_shapes=[
            pltpu.VMEM((FIELDS, ROWS, COLS), f32), pltpu.VMEM(states.shape, f32), dma((2, FIELDS + 1))
        ],
        compiler_params=pltpu.CompilerParams(vmem_limit_bytes=60 * 2**20),
        name="hand_over",
    )(points, states)


def solution(mesh):
    placed = (
        P("tm", None, "space", None),
        P(None, "space", None),
        P("tm", None, None, "space", None),
        P("space", None),
        P(),
        P("space", None),
        P("space", None),
        P("space", None),
        P("space"),
    )
    return jax.shard_map(
        per_device,
        mesh=mesh,
        in_specs=placed,
        out_specs=(P("tm", None, "space", None), P("tm", None, "space")),
        check_vma=False,
    )
```

```python
import jax
import jax.numpy as jnp
from jax import lax
from jax.experimental import pallas as pl
from jax.experimental.pallas import tpu as pltpu
from jax.sharding import PartitionSpec as P

STEPS = 4
ACT = 4
FIELDS = 5
ROWS = 64
COLS = 512
LANES = 128
BLOCKS = COLS // LANES
EDGE = 16
EXT = ROWS + 2 * EDGE
PIECE = 16
PIECES = ROWS // PIECE
GROUP = STEPS * ACT
SETS = 2 * STEPS
RIM = 4
INNER = ROWS - 2 * RIM
MESH = pl.DeviceIdType.MESH
LEVELS = 32767.0
f32 = jnp.float32
bf16 = jnp.bfloat16


def pair(ref, f, b, rows, shift):
    return jnp.concatenate([ref[f, b, pl.ds(row + shift, 8), :] for row in rows], axis=0)


def step_map(src, cond, rows, coupling, lane):
    first, last = lane == 0, lane == LANES - 1
    none = jnp.zeros(lane.shape, bf16)
    left, right = {}, {}
    for f in range(FIELDS):
        for b in range(BLOCKS):
            short = pair(src, f, b, rows, 0).astype(bf16)
            left[f, b] = pltpu.roll(short, 1, 1)
            right[f, b] = pltpu.roll(short, LANES - 1, 1)
    result = [[None] * BLOCKS for _ in range(FIELDS)]
    for b in range(BLOCKS):
        weight = jnp.concatenate([cond[b, pl.ds(row, 8), :] for row in rows], axis=0)
        keep, from_north, from_south, from_side = 1.0 - weight, 0.35 * weight, 0.15 * weight, 0.1 * weight
        mixed = []
        for f in range(FIELDS):
            west = jnp.where(first, left[f, b - 1] if b else none, left[f, b])
            east = jnp.where(last, right[f, b + 1] if b < BLOCKS - 1 else none, right[f, b])
            side = (jnp.bfloat16(3.0) * west + jnp.bfloat16(2.0) * east).astype(f32)
            mixed.append(
                keep * pair(src, f, b, rows, 0) + from_north * pair(src, f, b, rows, -1)
                + from_south * pair(src, f, b, rows, 1) + from_side * side
            )
        for f in range(FIELDS):
            total = coupling[0][f] * mixed[0]
            for g in range(1, FIELDS):
                total = total + coupling[g][f] * mixed[g]
            result[f][b] = total
    return result


def space_offsets(ns):
    nc = 2
    nx = min(4, ns // nc)
    ny = ns // (nc * nx)
    far = lambda d, n: min(d, n - d)
    steps = [(y, x, c) for y in range(ny) for x in range(nx) for c in range(nc)][1:]
    steps.sort(key=lambda o: -(2 * far(o[0], ny) + 2 * far(o[1], nx) + o[2]))
    return steps, (ny, nx, nc)


def time_offsets(nt):
    return sorted(range(1, nt), key=lambda j: -min(j, nt - j))


def offsets(distances, n):
    return sorted({d % n for d in distances} - {0})


def whole(
    points_in, terminal, forcing, conductance, coupling_ref, cells_in, acts_in, area_in, rate_ref,
    points, states,
    free, forced, push, cond, force_own, force_rows, force_out, force_in,
    start_out, start_in, end_out, end_in, cells, acts, area,
    coded, coded_scale, got, got_scale,
    column, row_inner, row_rim, inner, rim, picked, picked_rim, partial, mine, later, later_weight, send, result_rows,
    in_sem, z_send, z_recv, s_send, s_recv, a_send, a_recv, t_send, t_recv,
    greet_y, greet_far, greet_farther,
):
    nt, ns = lax.axis_size("tm"), lax.axis_size("space")
    t, s = lax.axis_index("tm"), lax.axis_index("space")
    around, (ny, nx, nc) = space_offsets(ns)
    place = (s // (nx * nc), lax.rem(s // nc, nx), lax.rem(s, nc))
    has_up, has_down = s < ns - 1, s > 0
    has_later, has_earlier = t < nt - 1, t > 0
    is_last = jnp.logical_not(has_later)

    def beside(o):
        y, x = lax.rem(place[0] + o[0], ny), lax.rem(place[1] + o[1], nx)
        c = 1 - place[2] if o[2] else place[2]
        return (t, (y * nx + x) * nc + c)

    def inverse(o):
        return around.index(((-o[0]) % ny, (-o[1]) % nx, o[2]))

    def in_time(j):
        return (lax.rem(t + j, nt), s)

    def signal(sem, dev):
        pl.semaphore_signal(sem, inc=1, device_id=dev, device_id_type=MESH)

    own = pl.ds(EDGE, ROWS)

    def load(src, dst, i):
        return pltpu.make_async_copy(src, dst, in_sem.at[i])

    def columns(src, dst, i):
        return [
            load(
                src.at[..., pl.ds(b * LANES, LANES)],
                dst.at[:, b, own, :] if len(dst.shape) == 4 else dst.at[b, own, :], i + b,
            )
            for b in range(BLOCKS)
        ]

    first_loads = columns(points_in.at[0], free.at[0], 0) + columns(conductance, cond, 4)
    force_load = load(forcing.at[0], force_own, 8)
    slot_loads = [load(cells_in, cells, 9), load(acts_in, acts, 10), load(area_in, area, 11)]
    end_loads = columns(terminal, forced.at[0], 12)
    for copy in slot_loads + [force_load] + first_loads[BLOCKS:] + first_loads[:BLOCKS]:
        copy.start()

    @pl.when(is_last)
    def _():
        for copy in end_loads:
            copy.start()

    later[...] = jnp.zeros(later.shape, f32)
    barrier = pltpu.get_barrier_semaphore()
    near_time = offsets((1, -1, 2, -2), nt)
    near_space = [o for o in around if o[0] == 0 or o[1:] == (0, 0)]
    for j in near_time:
        signal(barrier, in_time(j))
    signal(barrier, (t, lax.rem(s + 1, ns)))
    signal(barrier, (t, lax.rem(s + ns - 1, ns)))
    for o in near_space:
        signal(barrier, beside(o))

    lane16 = lax.broadcasted_iota(jnp.int32, (16, LANES), 1)
    lane1 = lax.broadcasted_iota(jnp.int32, (1, LANES), 1)
    coupling = [[coupling_ref[g, f] for f in range(FIELDS)] for g in range(FIELDS)]

    def advance(src, add, dst, rows):
        value = step_map(src, cond, rows, coupling, lane16)
        for f in range(FIELDS):
            for b in range(BLOCKS):
                for half, row in enumerate(rows):
                    part = value[f][b][8 * half : 8 * half + 8]
                    if add is not None:
                        part = part + add[f, b, pl.ds(row, 8), :]
                    dst[f, b, pl.ds(row, 8), :] = part

    def interior(src, add, dst, j, beside=None):
        per = 2 if beside is None else 4

        def body(i, carry):
            for tile in [per * i + n for n in range(per)]:
                if beside is not None:
                    beside(tile)
                row = jnp.minimum(EDGE + j + 16 * tile, EDGE + ROWS - j - 16)
                advance(src, add, dst, (row, row + 8))
            return carry

        lax.fori_loop(0, ROWS // 16 // per, body, 0)

    def edges(src, add, dst, j):
        advance(src, add, dst, (EDGE - 4 + j, EDGE + ROWS - 4 - j))

    for copy in slot_loads:
        copy.wait()

    numbers = lax.broadcasted_iota(jnp.int32, (COLS, LANES), 0).astype(jnp.int16)
    one, zero = jnp.ones((16, LANES), bf16), jnp.zeros((16, LANES), bf16)

    def slots(p, carry):
        for half in range(2):
            cell = cells[pl.ds(2 * p + half, 1), :]
            lanes = pl.ds(half * LANES, LANES)
            col = jnp.broadcast_to(jnp.bitwise_and(cell, COLS - 1), (16, LANES)).astype(jnp.int16)
            for at in range(0, COLS, 16):
                column[p, pl.ds(at, 16), lanes] = jnp.where(col == numbers[at : at + 16], one, zero)
            row = jnp.broadcast_to(lax.shift_right_arithmetic(cell, 9), (INNER, LANES))
            weight = jnp.broadcast_to(area[pl.ds(2 * p + half, 1), :], (INNER, LANES))
            at = lax.broadcasted_iota(jnp.int32, (INNER, LANES), 0) + RIM
            row_inner[p, :, lanes] = jnp.where(row == at, weight, 0.0)
            at = lax.broadcasted_iota(jnp.int32, (2 * RIM, LANES), 0)
            at = jnp.where(at < RIM, at, at + INNER)
            row_rim[p, :, lanes] = jnp.where(row[: 2 * RIM] == at, weight[: 2 * RIM], 0.0)
        return carry

    lax.fori_loop(0, ns // 2, slots, 0)


    force_load.wait()
    def widen(i, carry):
        k, f = i // FIELDS, lax.rem(i, FIELDS)
        value = force_own[k, f].astype(f32)
        for b in range(BLOCKS):
            push[k, f, b, own, :] = value[:, b * LANES : (b + 1) * LANES]
        return carry

    lax.fori_loop(0, STEPS * FIELDS, widen, 0)

    needs = ((3, 3, 0), (2, 2, 3), (1, 1, 5))
    near = (EDGE + ROWS, EDGE)
    for side in range(2):
        for b in range(BLOCKS):
            for f in range(FIELDS):
                for k, count, at in needs:
                    row = near[side] - count if side == 0 else near[side]
                    force_rows[side, b, pl.ds(6 * f + at, count), :] = push[k, f, b, pl.ds(row, count), :]
            force_rows[side, b, pl.ds(6 * FIELDS, 2), :] = jnp.zeros((2, LANES), f32)
            force_out[side, b] = force_rows[side, b].astype(bf16)

    def pack(ref, out):
        for side in range(2):
            row = near[side] - 4 if side == 0 else near[side]
            for b in range(BLOCKS):
                for f in range(FIELDS):
                    out[side, b, pl.ds(4 * f, 4), :] = ref[f, b, pl.ds(row, 4), :]
                out[side, b, pl.ds(4 * FIELDS, 4), :] = jnp.zeros((4, LANES), f32)

    def unpack(got_rows, ref):
        for side in range(2):
            row = EDGE - 4 if side == 0 else EDGE + ROWS
            for b in range(BLOCKS):
                for f in range(FIELDS):
                    ref[f, b, pl.ds(row, 4), :] = got_rows[side, b, pl.ds(4 * f, 4), :]

    for side, has, row in ((0, has_down, 8), (1, has_up, EDGE + ROWS)):
        @pl.when(jnp.logical_not(has))
        def _(side=side, row=row):
            start_in[side] = jnp.zeros(start_in.shape[1:], f32)
            end_in[side] = jnp.zeros(end_in.shape[1:], f32)
            cond[:, pl.ds(row, 8), :] = jnp.zeros((BLOCKS, 8, LANES), f32)
            force_in[side] = jnp.zeros(force_in.shape[1:], bf16)

    for copy in first_loads[BLOCKS:]:
        copy.wait()

    @pl.when(is_last)
    def _():
        for copy in end_loads:
            copy.wait()

    @pl.when(has_later)
    def _():
        forced[1, :, :, own, :] = push[3, :, :, own, :]

    @pl.when(is_last)
    def _():
        pack(forced.at[0], end_out)
        interior(forced.at[0], push.at[3], forced.at[1], 1)

    parts = (forced, free)

    def two_terms(value):
        high = value.astype(bf16).astype(f32)
        return jnp.concatenate([high, value - high], axis=0).astype(bf16)

    def fill_inner(part, stages):
        for stage in stages:
            value = jnp.concatenate(
                [parts[part][stage, 4, b, pl.ds(EDGE + RIM, INNER), :] for b in range(BLOCKS)], axis=1
            )
            at = 2 * INNER * (part * STEPS + STEPS - stage)
            inner[pl.ds(at, 2 * INNER), :] = two_terms(value)

    def pick(p, terms, first, sets, rows, weight, to):
        out = jnp.dot(
            terms[pl.ds(2 * rows * first, 2 * rows * sets), :], column[p], preferred_element_type=f32
        )
        for k in range(sets):
            at = 2 * k * rows
            both = (out[at : at + rows] + out[at + rows : at + 2 * rows]) * weight[p]
            line = jnp.sum(both, axis=0, keepdims=True)
            for half in range(2):
                to[first + k, pl.ds(2 * p + half, 1), :] = line[:, half * LANES : (half + 1) * LANES]

    def pick_inner(first, sets, p):
        pick(p, inner, first, sets, INNER, row_inner, picked)

    pairs = ns // 2

    def share(first, sets, turns):
        count = -(-pairs // turns)

        def turn(i):
            for n in range(count):
                if pairs == turns * count:
                    pick_inner(first, sets, count * i + n)

        return turn if pairs == turns * count else None

    def rest(first, sets, turns):
        if share(first, sets, turns) is None:
            for p in range(pairs):
                pick_inner(first, sets, p)

    tiles = ROWS // 16
    fill_inner(0, (1,))
    first_share = share(3, 1, 2 * tiles)
    interior(forced.at[1], push.at[2], forced.at[2], 2, first_share)
    for copy in first_loads[:BLOCKS]:
        copy.wait()
    pack(free.at[0], start_out)
    pl.semaphore_wait(barrier, len(near_time) + 2 + len(near_space))

    def s_copy(src, dst, i, to):
        return pltpu.make_async_remote_copy(
            src_ref=src, dst_ref=dst, send_sem=s_send.at[i], recv_sem=s_recv.at[i],
            device_id=(t, to), device_id_type=MESH,
        )

    def halo(side):
        to = s + 1 if side == 0 else s - 1
        mine_rows = pl.ds(EDGE + ROWS - 8 if side == 0 else EDGE, 8)
        their_rows = pl.ds(8 if side == 0 else EDGE + ROWS, 8)
        i = 4 * side
        return [
            s_copy(start_out.at[side], start_in.at[side], i, to),
            s_copy(cond.at[:, mine_rows, :], cond.at[:, their_rows, :], i + 1, to),
            s_copy(force_out.at[side], force_in.at[side], i + 2, to),
            s_copy(end_out.at[side], end_in.at[side], i + 3, to),
        ]

    up, down = halo(0), halo(1)
    for has, copies in ((has_up, up), (has_down, down)):
        @pl.when(has)
        def _(copies=copies):
            for copy in copies[:3]:
                copy.start()

        @pl.when(jnp.logical_and(has, is_last))
        def _(copies=copies):
            copies[3].start()

    same_x = [o for o in near_space if o[1:] == (0, 0)]
    for o in same_x:
        signal(greet_y, beside(o))
    far = offsets((2, -2), nt)
    for j in far:
        signal(greet_far, in_time(j))

    def shifted(turn, by):
        return None if turn is None else lambda i: turn(i + by)

    interior(forced.at[2], push.at[1], forced.at[3], 3, shifted(first_share, tiles))
    interior(forced.at[3], push.at[0], forced.at[4], 4)
    rest(3, 1, 2 * tiles)
    fill_inner(0, (2, 3, 4))
    second_share = share(0, 3, 2 * tiles)
    interior(free.at[0], None, free.at[1], 1, second_share)
    interior(free.at[1], None, free.at[2], 2, shifted(second_share, tiles))
    rest(0, 3, 2 * tiles)
    fill_inner(1, (1, 2))
    third_share = share(STEPS + 2, 2, 2 * tiles)
    interior(free.at[2], None, free.at[3], 3, third_share)
    interior(free.at[3], None, free.at[4], 4, shifted(third_share, tiles))
    rest(STEPS + 2, 2, 2 * tiles)
    fill_inner(1, (3, 4))

    pl.semaphore_wait(greet_far, len(far))
    farther = offsets((4, -4), nt)
    for j in farther:
        signal(greet_farther, in_time(j))

    for has, copies in ((has_down, up), (has_up, down)):
        @pl.when(has)
        def _(copies=copies):
            for copy in copies[:3]:
                copy.wait_recv()

        @pl.when(jnp.logical_and(has, is_last))
        def _(copies=copies):
            copies[3].wait_recv()

    unpack(start_in, free.at[0])
    for side in range(2):
        for b in range(BLOCKS):
            force_rows[side, b] = force_in[side, b].astype(f32)
            for f in range(FIELDS):
                for k, count, at in needs:
                    row = EDGE - count if side == 0 else EDGE + ROWS
                    push[k, f, b, pl.ds(row, count), :] = force_rows[side, b, pl.ds(6 * f + at, count), :]

    todo = [0]

    def some_free():
        todo[0] += 1
        for p in range((todo[0] - 1) * pairs // 7, todo[0] * pairs // 7):
            pick_inner(STEPS, 2, p)

    for j in range(1, STEPS + 1):
        some_free()
        edges(free.at[j - 1], None, free.at[j], j)

    for piece in range(PIECES):
        tile = []
        for f in range(FIELDS):
            x = free[STEPS, f, :, pl.ds(EDGE + piece * PIECE, PIECE), :]
            top = jnp.max(jnp.abs(x), axis=(0, 1, 2), keepdims=True)
            safe = jnp.maximum(top, 1e-30)
            y = jnp.round(x * (LEVELS / safe))
            coded[f, :, pl.ds(piece * PIECE, PIECE), :] = y.astype(jnp.int32).astype(jnp.int16)
            tile.append(jnp.broadcast_to(safe[0] * (1.0 / LEVELS), (1, LANES)))
        tile += [jnp.zeros((1, LANES), f32)] * (8 - FIELDS)
        coded_scale[piece] = jnp.concatenate(tile, axis=0)

    def z_copy(src, dst, i):
        return pltpu.make_async_remote_copy(
            src_ref=src, dst_ref=dst, send_sem=z_send.at[i], recv_sem=z_recv.at[i],
            device_id=(t - 1, s), device_id_type=MESH,
        )

    z_copies = [z_copy(coded_scale, got_scale, 0), z_copy(coded, got, 1)]

    @pl.when(has_earlier)
    def _():
        for copy in z_copies:
            copy.start()

    @pl.when(has_later)
    def _():
        for row, count, at in ((EDGE - 3, 3, 0), (EDGE + ROWS, 3, 0)):
            forced[1, :, :, pl.ds(row, count), :] = push[3, :, :, pl.ds(row, count), :]

    @pl.when(is_last)
    def _():
        unpack(end_in, forced.at[0])
        edges(forced.at[0], push.at[3], forced.at[1], 1)

    for j in range(2, STEPS + 1):
        some_free()
        edges(forced.at[j - 1], push.at[STEPS - j], forced.at[j], j)

    for part, ref in enumerate(parts):
        for k in range(STEPS):
            value = jnp.concatenate(
                [
                    jnp.concatenate(
                        [ref[STEPS - k, 4, b, pl.ds(EDGE, RIM), :],
                         ref[STEPS - k, 4, b, pl.ds(EDGE + ROWS - RIM, RIM), :]], axis=0
                    )
                    for b in range(BLOCKS)
                ],
                axis=1,
            )
            rim[pl.ds(4 * RIM * (part * STEPS + k), 4 * RIM), :] = two_terms(value)

    def pick_rim(p, carry):
        pick(p, rim, 0, SETS, 2 * RIM, row_rim, picked_rim)
        return carry

    lax.fori_loop(0, pairs, pick_rim, 0, unroll=pairs)
    ids = acts[...]
    wide = jnp.bitwise_and(lax.broadcasted_iota(jnp.int32, ids.shape, 1), 2 * GROUP - 1)
    total = jnp.zeros(ids.shape, f32)
    for k in range(SETS):
        values = picked[k] + picked_rim[k]
        for a in range(ACT):
            part = jnp.sum(jnp.where(ids == a, values, 0.0), axis=1, keepdims=True)
            total = jnp.where(wide == k * ACT + a, part, total)
    partial[...] = total.reshape(partial.shape)

    pl.semaphore_wait(greet_y, len(same_x))
    to_owner = []
    for i, o in enumerate(around):
        dev = beside(o)
        to_owner.append(pltpu.make_async_remote_copy(
            src_ref=partial.at[dev[1]], dst_ref=mine.at[inverse(o)],
            send_sem=a_send.at[i], recv_sem=a_recv.at[inverse(o)],
            device_id=dev, device_id_type=MESH,
        ))
    for copy in to_owner:
        copy.start()
    mine[ns - 1] = partial[s]

    rate = jnp.zeros((1, LANES), f32)
    for a in range(ACT):
        rate = jnp.where(lax.rem(lane1, ACT) == a, rate_ref[a], rate)
    k_of = lax.rem(lane1, GROUP) // ACT
    k_f = k_of.astype(f32)
    q_of = lane1 // GROUP
    decay = [jnp.exp(-float(m) * rate) for m in range(STEPS)]
    later_weight[0] = jnp.zeros((1, LANES), f32)
    for j in range(1, nt):
        forced_part = jnp.exp(-float(STEPS * (j - 1)) * rate)
        start_part = jnp.exp(-float(STEPS * (j - 2)) * rate) if j > 1 else 0.0
        row = jnp.where(q_of == 0, forced_part, 0.0) + jnp.where(q_of == 1, start_part, 0.0)
        if j == 1:
            row = row + jnp.where(q_of == 5, 1.0, 0.0)
        later_weight[j] = row
    pl.semaphore_wait(greet_farther, len(farther))
    for i, o in enumerate(around):
        pltpu.make_async_remote_copy(
            src_ref=partial.at[s], dst_ref=mine.at[i], send_sem=a_send.at[i], recv_sem=a_recv.at[i],
            device_id=beside(o), device_id_type=MESH,
        ).wait_recv()
    loads = jnp.sum(mine[...], axis=0)
    summed = loads * jnp.exp(-k_f * rate)
    for shift, low in ((8, k_of < 2), (4, lax.rem(k_of, 2) == 0)):
        other = jnp.where(low, pltpu.roll(summed, LANES - shift, 1), pltpu.roll(summed, shift, 1))
        summed = summed + other
    send[...] = jnp.where(q_of < 4, summed, loads)

    to_earlier = {
        j: pltpu.make_async_remote_copy(
            src_ref=send, dst_ref=later.at[j], send_sem=t_send.at[j], recv_sem=t_recv.at[j],
            device_id=(t - j, s), device_id_type=MESH,
        )
        for j in time_offsets(nt)
    }
    for j, copy in to_earlier.items():
        pl.when(t >= j)(copy.start)

    @pl.when(has_later)
    def _():
        for copy in z_copies:
            copy.wait_recv()

    @pl.when(is_last)
    def _():
        got[...] = jnp.zeros(got.shape, jnp.int16)
        got_scale[...] = jnp.zeros(got_scale.shape, f32)

    for piece in range(PIECES):
        rows = pl.ds(piece * PIECE, PIECE)
        for f in range(FIELDS):
            factor = got_scale[piece, f : f + 1, :]
            for b in range(BLOCKS):
                value = got[f, b, rows, :].astype(jnp.int32).astype(f32) * factor
                result_rows[f, rows, pl.ds(b * LANES, LANES)] = (
                    value + forced[STEPS, f, b, pl.ds(EDGE + piece * PIECE, PIECE), :]
                )

    store = load(result_rows, points.at[0], 8)
    store.start()
    for j, copy in to_earlier.items():
        pl.when(t + j < nt)(copy.wait_recv)
    arrived = jnp.sum(later[...] * later_weight[...], axis=0)
    loads = loads + pltpu.roll(arrived, LANES - 5 * GROUP, 1)
    incoming = arrived + pltpu.roll(arrived, LANES - GROUP, 1)
    result = loads + jnp.exp(-(STEPS - k_f) * rate) * incoming
    for m in range(1, STEPS):
        moved = pltpu.roll(loads, LANES - ACT * m, 1)
        result = result + jnp.where(k_of + m < STEPS, decay[m] * moved, 0.0)
    for k in range(STEPS):
        moved = pltpu.roll(result, LANES - ACT * k, 1) if k else result
        states[0, pl.ds(k, 1), :] = moved[:, :ACT]

    store.wait()
    for j, copy in to_earlier.items():
        pl.when(t >= j)(copy.wait_send)
    for copy in to_owner:
        copy.wait_send()
    for has, copies in ((has_up, up), (has_down, down)):
        @pl.when(has)
        def _(copies=copies):
            for copy in copies[:3]:
                copy.wait_send()

        @pl.when(jnp.logical_and(has, is_last))
        def _(copies=copies):
            copies[3].wait_send()

    @pl.when(has_earlier)
    def _():
        for copy in z_copies:
            copy.wait_send()


def hand_over(points_in, states_in, points, states, rows, small, sem):
    into = [
        pltpu.make_async_copy(points_in.at[0, f], rows.at[f], sem.at[0, f]) for f in range(FIELDS)
    ] + [pltpu.make_async_copy(states_in, small, sem.at[0, FIELDS])]
    out = [
        pltpu.make_async_copy(rows.at[f], points.at[0, f], sem.at[1, f]) for f in range(FIELDS)
    ] + [pltpu.make_async_copy(small, states, sem.at[1, FIELDS])]
    for copy in into:
        copy.start()
    for first, then in zip(into, out):
        first.wait()
        then.start()
    for copy in out:
        copy.wait()


def per_device(
    c_points, terminal, forcing, conductance, coupling, flap_cells, flap_actuator, flap_area, actuator_rate
):
    nt, ns = lax.axis_size("tm"), lax.axis_size("space")
    anywhere = pl.BlockSpec(memory_space=pl.ANY)
    vmem = pl.BlockSpec(memory_space=pltpu.VMEM)
    smem = pl.BlockSpec(memory_space=pltpu.SMEM)
    dma = pltpu.SemaphoreType.DMA
    regular = pltpu.SemaphoreType.REGULAR
    i32 = jnp.int32
    block = (FIELDS, BLOCKS, EXT, LANES)
    points, states = pl.pallas_call(
        whole,
        out_shape=(
            jax.ShapeDtypeStruct((1, FIELDS, ROWS, COLS), f32),
            jax.ShapeDtypeStruct((1, STEPS, ACT), f32),
        ),
        in_specs=[anywhere] * 4 + [smem] + [anywhere] * 3 + [smem],
        out_specs=(anywhere, vmem),
        scratch_shapes=[
            pltpu.VMEM((STEPS + 1,) + block, f32),
            pltpu.VMEM((STEPS + 1,) + block, f32),
            pltpu.VMEM((STEPS,) + block, f32),
            pltpu.VMEM(block[1:], f32),
            pltpu.VMEM((STEPS, FIELDS, ROWS, COLS), bf16),
            pltpu.VMEM((2, BLOCKS, 32, LANES), f32),
            pltpu.VMEM((2, BLOCKS, 32, LANES), bf16),
            pltpu.VMEM((2, BLOCKS, 32, LANES), bf16),
            pltpu.VMEM((2, BLOCKS, 24, LANES), f32),
            pltpu.VMEM((2, BLOCKS, 24, LANES), f32),
            pltpu.VMEM((2, BLOCKS, 24, LANES), f32),
            pltpu.VMEM((2, BLOCKS, 24, LANES), f32),
            pltpu.VMEM((ns, LANES), i32),
            pltpu.VMEM((ns, LANES), i32),
            pltpu.VMEM((ns, LANES), f32),
            pltpu.VMEM((FIELDS, BLOCKS, ROWS, LANES), jnp.int16),
            pltpu.VMEM((PIECES, 8, LANES), f32),
            pltpu.VMEM((FIELDS, BLOCKS, ROWS, LANES), jnp.int16),
            pltpu.VMEM((PIECES, 8, LANES), f32),
            pltpu.VMEM((ns // 2, COLS, 2 * LANES), bf16),
            pltpu.VMEM((ns // 2, INNER, 2 * LANES), f32),
            pltpu.VMEM((ns // 2, 2 * RIM, 2 * LANES), f32),
            pltpu.VMEM((2 * SETS * INNER, COLS), bf16),
            pltpu.VMEM((4 * SETS * RIM, COLS), bf16),
            pltpu.VMEM((SETS, ns, LANES), f32),
            pltpu.VMEM((SETS, ns, LANES), f32),
            pltpu.VMEM((ns, 1, LANES), f32),
            pltpu.VMEM((ns, 1, LANES), f32),
            pltpu.VMEM((nt, 1, LANES), f32),
            pltpu.VMEM((nt, 1, LANES), f32),
            pltpu.VMEM((1, LANES), f32),
            pltpu.VMEM((FIELDS, ROWS, COLS), f32),
            dma((16,)), dma((2,)), dma((2,)), dma((8,)), dma((8,)),
            dma((ns,)), dma((ns,)), dma((nt,)), dma((nt,)),
            regular, regular, regular,
        ],
        compiler_params=pltpu.CompilerParams(
            collective_id=0, has_side_effects=True, vmem_limit_bytes=58 * 2**20
        ),
        name="whole",
    )(c_points, terminal, forcing, conductance, coupling, flap_cells, flap_actuator, flap_area, actuator_rate)
    return pl.pallas_call(
        hand_over,
        out_shape=(
            jax.ShapeDtypeStruct(points.shape, f32),
            jax.ShapeDtypeStruct(states.shape, f32),
        ),
        in_specs=[anywhere] * 2,
        out_specs=(anywhere,) * 2,
        scratch_shapes=[
            pltpu.VMEM((FIELDS, ROWS, COLS), f32), pltpu.VMEM(states.shape, f32), dma((2, FIELDS + 1))
        ],
        compiler_params=pltpu.CompilerParams(vmem_limit_bytes=60 * 2**20),
        name="hand_over",
    )(points, states)


def solution(mesh):
    placed = (
        P("tm", None, "space", None),
        P(None, "space", None),
        P("tm", None, None, "space", None),
        P("space", None),
        P(),
        P("space", None),
        P("space", None),
        P("space", None),
        P("space"),
    )
    return jax.shard_map(
        per_device,
        mesh=mesh,
        in_specs=placed,
        out_specs=(P("tm", None, "space", None), P("tm", None, "space")),
        check_vma=False,
    )
```
